256 devices in a mesh: row: 16 (over z, y_lo), col: 16 (over y_hi, x, core).
Axes of the slice: x: 4, y: 4 (y_hi: 2, y_lo: 2; y = y_hi * 2 + y_lo), z: 8, core: 2. Of those that a mesh axis runs over, the one named last changes fastest.
Arguments:
- factors: bfloat16 [768, 12, 5120], P('row', None, 'col'), may hold values from -0.21875 to 0.21875
- amplitudes: bfloat16 [16, 12, 12], replicated, may hold values from -6 to 6
- vir_energy: float32 [768], replicated, may hold values from 0.2 to 2
- pair_energy: float32 [16], replicated, may hold values from -1.5 to -0.5
Outputs:
- residual: float32 [16, 768, 768], P('col', 'row')
- update: float32 [16, 768, 768], P('col', 'row')
The draws below stay inside these ranges and needn't reach their ends.
All inputs are finite; a program needn't handle non-finite values.
Results may differ from the reference program's by a relative error of at most 0.0024.
Values may be sent and summed in bfloat16 or wider, within the bound.
No kernel may reach another device: no remote copies, remote signals or barrier semaphores. Data moves between devices by JAX's collectives and lax.ppermute only.
A program may use at most 256 MiB of HBM per device.

```python
import jax
import jax.numpy as jnp
from jax import lax

V = 768
Q = 5120
S = 12
P_SIZE = 16
VIR_ROW = 48
AUX_COL = 320
N_ROW = 16
N_COL = 16


def steps_of(rng, extent, cuts, smallest, top_value):
    level, own = 1.0, jax.random.fold_in(rng, 6)
    for axis_at, blocks in cuts:
        heights = jnp.exp(jax.random.uniform(jax.random.fold_in(own, axis_at), (blocks,), jnp.float32, smallest / len(cuts), top_value / len(cuts)))
        level = level * jnp.repeat(heights, extent[axis_at] // blocks).reshape([-1 if axis == axis_at else 1 for axis in range(len(extent))])
    return level


def gaussian(rng, dims, deviation, most, shards=(), kind=jnp.bfloat16):
    array = jax.random.normal(rng, dims, jnp.float32) * deviation
    if len(shards) > 0:
        array = steps_of(rng, dims, shards, -0.22, 0.18) * array
    return jnp.clip(array, min=-most, max=most).astype(kind)


def setup_inputs(seed: int = 0) -> dict:
    splits = jax.random.split(jax.random.key(seed), 5)
    return {
        "factors": gaussian(splits[0], (V, S, Q), ((S * Q ** 0.5) ** -0.5), 0.21875, ((0, 16), (2, 16))),
        "amplitudes": gaussian(splits[1], (P_SIZE, S, S), 1.0, 6.0),
        "vir_energy": jnp.clip(jax.random.uniform(splits[2], (V,), jnp.float32, 0.2, 2.0), 0.2, 2.0),
        "pair_energy": jnp.clip(jax.random.uniform(splits[3], (P_SIZE,), jnp.float32, -1.5, -0.5), -1.5, -0.5),
    }


def reference(factors, amplitudes, vir_energy, pair_energy):
    aux_blocks = jnp.transpose(factors.reshape(V, S, N_COL, AUX_COL), (2, 0, 1, 3))
    wide_amplitudes = amplitudes.astype(jnp.float32)

    def block_rows(row_index):
        def add_block(total, aux_index):
            right_block = aux_blocks[aux_index]
            slab_block = lax.dynamic_slice_in_dim(right_block, (row_index * VIR_ROW).astype(jnp.int32), VIR_ROW, 0)
            products = jnp.dot(slab_block.reshape(VIR_ROW * S, AUX_COL), right_block.reshape(V * S, AUX_COL).T, preferred_element_type=jnp.float32)
            products = products.astype(jnp.bfloat16).astype(jnp.float32).reshape(VIR_ROW, S, V, S)
            term = jnp.einsum('acbd,pcd->pab', products, wide_amplitudes, precision=lax.Precision.HIGHEST)
            return total + term, None

        start = jnp.zeros((P_SIZE, VIR_ROW, V), jnp.float32)
        total, _ = lax.scan(add_block, start, jnp.arange(N_COL, dtype=jnp.int32))
        return total

    pieces = lax.map(block_rows, jnp.arange(N_ROW, dtype=jnp.int32))
    residual = jnp.transpose(pieces, (1, 0, 2, 3)).reshape(P_SIZE, V, V)
    divisor = vir_energy[None, :, None] + vir_energy[None, None, :] - pair_energy[:, None, None]
    return residual, residual / divisor
```

```python
import jax
import jax.numpy as jnp
import numpy as np
from jax import lax
from jax.experimental import pallas as pl
from jax.experimental.pallas import tpu as pltpu
from jax.sharding import PartitionSpec as P

ROWS = 48
SLAB = 12
PAIRS = 16
LANE = 128
WIDE = 256
TILES = 30
GROUP = 8
GROUPS = ROWS // GROUP
DEPTH = SLAB * SLAB * GROUP
OUT = 3 * LANE
BF16 = jnp.bfloat16
F32 = jnp.float32


def device_of(index):
    row, col = divmod(index, 16)
    return row // 2, row % 2, col // 8, (col // 2) % 4, col % 2


def index_of(z, y_lo, y_hi, x, core):
    return ((z % 8) * 2 + y_lo % 2) * 16 + (y_hi % 2) * 8 + (x % 4) * 2 + core % 2


def shift(array, dz=0, dy=0, dh=0, dx=0, dc=0):
    pairs = []
    for source in range(256):
        z, y, h, x, c = device_of(source)
        pairs.append((source, index_of(z + dz, y + dy, h + dh, x + dx, c + dc)))
    return lax.ppermute(array, ("row", "col"), pairs)


def full(count):
    return [pl.BlockSpec(memory_space=pltpu.VMEM)] * count


def params():
    return pltpu.CompilerParams(vmem_limit_bytes=40 * 1024 * 1024)


def pack_block(factors):
    main = factors[:, :, :WIDE].reshape(ROWS, 2 * SLAB, LANE).transpose(1, 0, 2)
    rest = factors[:, :, WIDE:].reshape(ROWS, 2, SLAB // 2, LANE // 2)
    rest = rest.transpose(2, 0, 1, 3).reshape(SLAB // 2, ROWS, LANE)
    return jnp.concatenate([main, rest], axis=0)


def star_kernel(center, m1, own, p1, m2, p2, weights, keep, send, left, products):
    low = lax.broadcasted_iota(jnp.int32, (ROWS, LANE), 1) < LANE // 2
    zero = jnp.zeros((ROWS, LANE), F32)
    for c in range(SLAB):
        rows = pl.ds(c * ROWS, ROWS)
        last = center[2 * SLAB + c % 6].astype(F32)
        moved = pltpu.roll(last, LANE // 2, 1)
        in_low, in_high = (last, moved) if c < 6 else (moved, last)
        for half in range(2):
            left[half, rows, 0:LANE] = center[2 * c]
            left[half, rows, LANE:2 * LANE] = center[2 * c + 1]
        left[0, rows, 2 * LANE:] = jnp.where(low, in_low, zero).astype(BF16)
        left[1, rows, 2 * LANE:] = jnp.where(low, zero, in_high).astype(BF16)
    for d in range(SLAB):
        columns = []
        for tile in (2 * d, 2 * d + 1, 2 * SLAB + d % 6):
            columns.append(jnp.concatenate(
                [m1[tile], own[tile], p1[tile], m2[tile], p2[tile], p1[tile, 32:, :]], axis=0))
        right = jnp.concatenate(columns, axis=1)
        block = lax.dot_general(left[d // 6], right, (((1,), (1,)), ((), ())), preferred_element_type=F32)
        block = block.reshape(SLAB, GROUPS, GROUP, WIDE)
        for g in range(GROUPS):
            part = block[:, g].reshape(SLAB * GROUP, WIDE)
            products[g, d * SLAB * GROUP:(d + 1) * SLAB * GROUP, :] = part.astype(BF16)
    first = lax.broadcasted_iota(jnp.int32, (PAIRS * GROUP, LANE), 1) < 5 * ROWS - LANE
    half_pairs = PAIRS // 2
    for g in range(GROUPS):
        terms = jnp.dot(weights[...], products[g], preferred_element_type=F32)
        plain, mirror = terms[:PAIRS * GROUP], terms[PAIRS * GROUP:]
        middle = jnp.where(first, plain[:, LANE:], mirror[:, LANE:])
        rows = pl.ds(g * GROUP, GROUP)
        for at, value in enumerate((plain[:, :LANE], middle, mirror[:, :LANE])):
            value = value.reshape(PAIRS, GROUP, LANE)
            lanes = pl.ds(at * LANE, LANE)
            keep[:, rows, lanes] = value[:half_pairs]
            send[:, rows, lanes] = value[half_pairs:]


def star(center, others, weights):
    half = jax.ShapeDtypeStruct((PAIRS // 2, ROWS, OUT), F32)
    return pl.pallas_call(
        star_kernel,
        out_shape=(half, half),
        in_specs=full(7),
        out_specs=tuple(full(2)),
        scratch_shapes=[
            pltpu.VMEM((2, SLAB * ROWS, 3 * LANE), BF16),
            pltpu.VMEM((GROUPS, DEPTH, WIDE), BF16),
        ],
        compiler_params=params(),
        cost_estimate=pl.CostEstimate(flops=3_500_000_000, bytes_accessed=4_000_000, transcendentals=0),
        name="star",
    )(center, *others, weights)


def core_kernel(keep, got, stay, one, two, three):
    stay[...] = keep[0:2] + got[0:2]
    one[...] = (keep[2:4] + got[2:4]).astype(BF16)
    two[...] = (keep[4:6] + got[4:6]).astype(BF16)
    three[...] = (keep[6:8] + got[6:8]).astype(BF16)


def add_cores(keep, got):
    part = jax.ShapeDtypeStruct((2, ROWS, OUT), BF16)
    return pl.pallas_call(
        core_kernel,
        out_shape=(jax.ShapeDtypeStruct((2, ROWS, OUT), F32), part, part, part),
        in_specs=full(2),
        out_specs=tuple(full(4)),
        compiler_params=params(),
        name="add_cores",
    )(keep, got)


def x_kernel(stay, one, two, three, keep, send):
    total = stay[...] + one[...].astype(F32) + two[...].astype(F32) + three[...].astype(F32)
    keep[...] = total[0]
    send[...] = total[1].astype(BF16)


def add_x(*parts):
    return pl.pallas_call(
        x_kernel,
        out_shape=(jax.ShapeDtypeStruct((ROWS, OUT), F32), jax.ShapeDtypeStruct((ROWS, OUT), BF16)),
        in_specs=full(4),
        out_specs=tuple(full(2)),
        compiler_params=params(),
        name="add_x",
    )(*parts)


def y_kernel(keep_a, got_a, keep_b, got_b, plain_a, plain_b, to_m1, own, to_p1):
    sum_a = keep_a[...] + got_a[...].astype(F32)
    sum_b = keep_b[...] + got_b[...].astype(F32)
    plain_a[...] = sum_a[:, :WIDE]
    plain_b[...] = sum_b[:, :WIDE]
    pad = jnp.zeros((LANE - 2 * ROWS, LANE), F32)
    mirror = jnp.concatenate([sum_a[:, WIDE:], sum_b[:, WIDE:], pad], axis=0).T
    tail = jnp.concatenate([sum_a[:, LANE:WIDE], sum_b[:, LANE:WIDE], pad], axis=0).T
    to_m1[...] = mirror[0:ROWS]
    own[...] = mirror[ROWS:2 * ROWS]
    to_p1[0:32, :] = mirror[2 * ROWS:]
    to_p1[32:, :] = tail[LANE - 16:]


def add_y(*parts):
    wide = jax.ShapeDtypeStruct((ROWS, WIDE), F32)
    slim = jax.ShapeDtypeStruct((ROWS, LANE), F32)
    return pl.pallas_call(
        y_kernel,
        out_shape=(wide, wide, slim, slim, slim),
        in_specs=full(4),
        out_specs=tuple(full(5)),
        compiler_params=params(),
        name="add_y",
    )(*parts)


def place_kernel(plain_a, plain_b, from_p1, own, from_m1, places, divisor, residual, update):
    source = jnp.concatenate(
        [plain_a[...], plain_b[...], from_p1[...], own[...], from_m1[...]], axis=1)
    high = source.astype(BF16)
    rest = source - high.astype(F32)
    middle = rest.astype(BF16)
    low = (rest - middle.astype(F32)).astype(BF16)
    stacked = jnp.concatenate([high, middle, low], axis=0)
    placed = jnp.dot(stacked, places[...], preferred_element_type=F32)
    value = placed[:ROWS] + (placed[ROWS:2 * ROWS] + placed[2 * ROWS:])
    residual[0] = value
    update[0] = value / divisor[...]


def place(*parts):
    out = jax.ShapeDtypeStruct((1, ROWS, 16 * ROWS), F32)
    return pl.pallas_call(
        place_kernel,
        out_shape=(out, out),
        in_specs=full(7),
        out_specs=tuple(full(2)),
        compiler_params=params(),
        name="place",
    )(*parts)


def place_table():
    blocks = [[(1, 0), (2, 0), (3, 0), (0, 0), (4, 0)],
              [(5, 1), (6, 1), (7, 1), (4, 1), (0, 1)],
              [(7, 0), (3, 1)], [(6, 0), (2, 1)], [(5, 0), (1, 1)]]
    widths = [WIDE, WIDE, LANE, LANE, LANE]
    dz, dy, at, counts = [], [], [], []
    for group, width in zip(blocks, widths):
        for lane in range(width):
            valid = lane < ROWS * len(group)
            block = group[lane // ROWS] if valid else (0, 0)
            dz.append(block[0])
            dy.append(block[1])
            at.append(lane % ROWS)
            counts.append(valid)
    return np.array(dz, np.int32), np.array(dy, np.int32), np.array(at, np.int32), np.array(counts)


def contraction_weights(amplitudes, y_hi, x, core):
    plain = jnp.swapaxes(amplitudes, 1, 2).reshape(PAIRS, SLAB * SLAB)
    mirror = amplitudes.reshape(PAIRS, SLAB * SLAB)
    both = jnp.concatenate([plain, mirror], axis=0)
    row = jnp.arange(2 * PAIRS * GROUP, dtype=jnp.int32)
    near = (row // GROUP) % PAIRS
    order = row // (GROUP * PAIRS)
    pair = ((near % 2) ^ y_hi) * 8 + ((near // 2 + x) % 4) * 2 + ((near // 8) ^ core)
    chosen = (order * PAIRS + pair)[:, None] == jnp.arange(2 * PAIRS, dtype=jnp.int32)[None, :]
    spread = np.arange(DEPTH)[None, :] // GROUP == np.arange(SLAB * SLAB)[:, None]
    rows = jnp.dot(chosen.astype(BF16), both, preferred_element_type=F32).astype(BF16)
    wide = jnp.dot(rows, jnp.asarray(spread, BF16), preferred_element_type=F32)
    same = (row % GROUP)[:, None] == jnp.arange(DEPTH, dtype=jnp.int32)[None, :] % GROUP
    return jnp.where(same, wide, 0.0).astype(BF16)


def per_device(factors, amplitudes, vir_energy, pair_energy):
    here_row = lax.axis_index("row")
    here_col = lax.axis_index("col")
    z, y_lo = here_row // 2, here_row % 2
    y_hi, x, core = here_col // 8, (here_col // 2) % 4, here_col % 2

    own = pack_block(factors)
    p1 = shift(own, dz=-1)
    m1 = shift(own, dz=1)

    weights = contraction_weights(amplitudes, y_hi, x, core)
    dz, dy, at, counts = place_table()
    target = (((z + dz) % 8) * 2 + (y_lo ^ dy)) * ROWS + at
    places = (target[:, None] == jnp.arange(16 * ROWS, dtype=jnp.int32)[None, :]) & counts[:, None]
    places = places.astype(BF16)
    first_energy = lax.dynamic_slice_in_dim(vir_energy, here_row * ROWS, ROWS)
    pair_here = lax.dynamic_slice_in_dim(pair_energy, here_col, 1)
    divisor = first_energy[:, None] + vir_energy[None, :] - pair_here[:, None]

    p2 = shift(p1, dz=-1)
    m2 = shift(m1, dz=1)
    cross = shift(p2, dy=1)
    others = (m1, own, p1, m2, p2)

    def reduced(center):
        keep, send = star(center, others, weights)
        stay, one, two, three = add_cores(keep, shift(send, dc=1))
        keep, send = add_x(stay, shift(one, dx=1), shift(two, dx=2), shift(three, dx=-1))
        return keep, shift(send, dh=1)

    keep_a, got_a = reduced(m2)
    keep_b, got_b = reduced(cross)
    plain_a, plain_b, to_m1, stays, to_p1 = add_y(keep_a, got_a, keep_b, got_b)
    return place(
        shift(plain_a, dz=-2), shift(plain_b, dz=2, dy=1), shift(to_m1, dz=-1), stays, shift(to_p1, dz=1),
        places, divisor)


def solution(mesh):
    return jax.shard_map(
        per_device,
        mesh=mesh,
        in_specs=(P("row", None, "col"), P(), P(), P()),
        out_specs=(P("col", "row", None), P("col", "row", None)),
        check_vma=False,
    )
```

```python
import jax
import jax.numpy as jnp
import numpy as np
from jax import lax
from jax.experimental import pallas as pl
from jax.experimental.pallas import tpu as pltpu
from jax.sharding import PartitionSpec as P

ROWS = 48
SLAB = 12
PAIRS = 16
LANE = 128
WIDE = 256
CHUNK = 15
GROUP = 8
GROUPS = ROWS // GROUP
DEPTH = SLAB * SLAB * GROUP // 2
OUT = 3 * LANE
BF16 = jnp.bfloat16
F32 = jnp.float32


def device_of(index):
    row, col = divmod(index, 16)
    return row // 2, row % 2, col // 8, (col // 2) % 4, col % 2


def index_of(z, y_lo, y_hi, x, core):
    return ((z % 8) * 2 + y_lo % 2) * 16 + (y_hi % 2) * 8 + (x % 4) * 2 + core % 2


def shift(array, dz=0, dy=0, dh=0, dx=0, dc=0):
    pairs = []
    for source in range(256):
        z, y, h, x, c = device_of(source)
        pairs.append((source, index_of(z + dz, y + dy, h + dh, x + dx, c + dc)))
    return lax.ppermute(array, ("row", "col"), pairs)


def to_rows(array, flows):
    pairs = []
    for source in range(256):
        z, y, h, x, c = device_of(source)
        dz, dy = flows[c]
        pairs.append((source, index_of(z + dz, y + dy, h, x, c)))
    return lax.ppermute(array, ("row", "col"), pairs)


def full(count):
    return [pl.BlockSpec(memory_space=pltpu.VMEM)] * count


def params():
    return pltpu.CompilerParams(vmem_limit_bytes=24 * 1024 * 1024)


def core_here():
    return lax.rem(lax.axis_index("col"), 2)


def tiles_of(c):
    start, within = CHUNK * (c // 6), c % 6
    return start + 2 * within, start + 2 * within + 1, start + 12 + within % 3, within // 3


def pack_kernel(factors, packed):
    for c in range(SLAB):
        first, second, last, half = tiles_of(c)
        packed[first] = factors[c, :, 0:LANE]
        packed[second] = factors[c, :, LANE:WIDE]
        if half == 0:
            both = [factors[at, :, WIDE:].astype(F32) for at in (c, c + 3)]
            packed[last] = jnp.concatenate(both, axis=1).astype(BF16)


def pack_block(factors):
    return pl.pallas_call(
        pack_kernel,
        out_shape=jax.ShapeDtypeStruct((2 * CHUNK, ROWS, LANE), BF16),
        in_specs=full(1),
        out_specs=full(1)[0],
        compiler_params=params(),
        name="pack",
    )(jnp.transpose(factors, (1, 0, 2)))


def build_left(center, left):
    low = lax.broadcasted_iota(jnp.int32, (ROWS, LANE), 1) < LANE // 2
    zero = jnp.zeros((ROWS, LANE), F32)
    for c in range(SLAB):
        rows = pl.ds(c * ROWS, ROWS)
        main, second, tile, at = tiles_of(c)
        last = center[tile].astype(F32)
        moved = pltpu.roll(last, LANE // 2, 1)
        in_low, in_high = (last, moved) if at == 0 else (moved, last)
        for half in range(2):
            left[half, rows, 0:LANE] = center[main]
            left[half, rows, LANE:2 * LANE] = center[second]
        left[0, rows, 2 * LANE:] = jnp.where(low, in_low, zero).astype(BF16)
        left[1, rows, 2 * LANE:] = jnp.where(low, zero, in_high).astype(BF16)


def build_products(left, near, own, far, m2, p2, products):
    rows = 6 * GROUP
    for d in range(SLAB):
        columns = []
        first, second, last, half = tiles_of(d)
        for tile in (first, second, last):
            columns.append(jnp.concatenate(
                [near[tile], own[tile], far[tile], m2[tile], p2[tile], far[tile, 32:, :]], axis=0))
        right = jnp.concatenate(columns, axis=1)
        block = lax.dot_general(left[half], right, (((1,), (1,)), ((), ())), preferred_element_type=F32)
        block = block.reshape(2, 6, GROUPS, GROUP, WIDE)
        for chunk in range(2):
            for g in range(GROUPS):
                part = block[chunk, :, g].reshape(rows, WIDE)
                products[chunk, g, d * rows:(d + 1) * rows, :] = part.astype(BF16)


def contract(one, two, products, g):
    return (jnp.dot(one[...], products[0, g], preferred_element_type=F32)
            + jnp.dot(two[...], products[1, g], preferred_element_type=F32))


def first_kernel(center, m1, own, p1, m2, p2, one, two, energy, pair, raw, divisor, left, products):
    shape = divisor.shape
    second = jnp.broadcast_to(energy[...], shape)
    row = lax.axis_index("row") * ROWS + lax.broadcasted_iota(jnp.int32, shape, 0)
    mine = lax.broadcasted_iota(jnp.int32, shape, 1) == row
    first = jnp.sum(jnp.where(mine, second, 0.0), axis=1, keepdims=True)
    divisor[...] = first + second - pair[lax.axis_index("col")]
    build_left(center, left)
    build_products(left, m1, own, p1, m2, p2, products)
    for g in range(GROUPS):
        raw[g] = contract(one, two, products, g)


def second_kernel(center, m1, own, p1, m2, p2, one, two, raw, keep, send, left, products):
    build_left(center, left)
    build_products(left, p1, own, m1, m2, p2, products)
    half = PAIRS * GROUP
    lane = lax.broadcasted_iota(jnp.int32, (half, LANE), 1)
    here = core_here() == 0
    shape = (2, 4, 2, GROUP, LANE)
    for g in range(0, GROUPS, 2):
        staying, going = [], []
        for step in range(2):
            mine = contract(one, two, products, g + step)
            other = raw[g + step]
            for at, inside in enumerate((LANE, 5 * ROWS - LANE, 2 * ROWS)):
                lanes = slice(LANE, WIDE) if at == 1 else slice(0, LANE)
                row = slice(half, 2 * half) if at == 2 else slice(0, half)
                back = slice(half, 2 * half)
                down, up = other[row, lanes], mine[row, lanes]
                if at > 0:
                    down, up = (jnp.where(lane < inside, down, mine[back, lanes]),
                                jnp.where(lane < inside, up, other[back, lanes]))
                staying.append(jnp.where(here, down, up).reshape(shape))
                going.append(jnp.where(here, up, down).reshape(shape))
        rows = pl.ds(g * GROUP, 2 * GROUP)
        for at in range(3):
            lanes = pl.ds(at * LANE, LANE)
            keep[:, :, :, rows, lanes] = jnp.concatenate([staying[at], staying[3 + at]], axis=3)
            send[:, :, :, rows, lanes] = jnp.concatenate([going[at], going[3 + at]], axis=3).astype(BF16)


def scratch():
    return [
        pltpu.VMEM((2, SLAB * ROWS, 3 * LANE), BF16),
        pltpu.VMEM((2, GROUPS, DEPTH, WIDE), BF16),
    ]


def first_star(center, others, weights, vir_energy, pair_energy):
    return pl.pallas_call(
        first_kernel,
        out_shape=(jax.ShapeDtypeStruct((GROUPS, 2 * PAIRS * GROUP, WIDE), F32),
                   jax.ShapeDtypeStruct((ROWS, 16 * ROWS), F32)),
        in_specs=full(9) + [pl.BlockSpec(memory_space=pltpu.SMEM)],
        out_specs=tuple(full(2)),
        scratch_shapes=scratch(),
        compiler_params=params(),
        name="first_star",
    )(center, *others, *weights, vir_energy[None, :], pair_energy)


def second_star(center, others, weights, raw):
    shape = (2, 4, 2, ROWS, OUT)
    return pl.pallas_call(
        second_kernel,
        out_shape=(jax.ShapeDtypeStruct(shape, F32), jax.ShapeDtypeStruct(shape, BF16)),
        in_specs=full(9),
        out_specs=tuple(full(2)),
        scratch_shapes=scratch(),
        compiler_params=params(),
        name="second_star",
    )(center, *others, *weights, raw)


def core_kernel(keep, got, stay, one, two, three):
    x = lax.rem(lax.div(lax.axis_index("col"), 2), 4)
    for step, out in enumerate((stay, one, two, three)):
        at = lax.rem(x + step, 4)
        out[...] = (keep[:, at] + got[:, at].astype(F32)).astype(out.dtype)


def add_cores(keep, got):
    shape = (2, 2, ROWS, OUT)
    return pl.pallas_call(
        core_kernel,
        out_shape=(jax.ShapeDtypeStruct(shape, F32),) + (jax.ShapeDtypeStruct(shape, BF16),) * 3,
        in_specs=full(2),
        out_specs=tuple(full(4)),
        compiler_params=params(),
        name="add_cores",
    )(keep, got)


def x_kernel(stay, two, three, one, keep, send):
    y_hi = lax.div(lax.axis_index("col"), 8)
    for at, out in ((y_hi, keep), (1 - y_hi, send)):
        total = stay[at] + one[at].astype(F32) + two[at].astype(F32) + three[at].astype(F32)
        out[...] = total.astype(out.dtype)


def add_x(*parts):
    shape = (2, ROWS, OUT)
    return pl.pallas_call(
        x_kernel,
        out_shape=(jax.ShapeDtypeStruct(shape, F32), jax.ShapeDtypeStruct(shape, BF16)),
        in_specs=full(4),
        out_specs=tuple(full(2)),
        compiler_params=params(),
        name="add_x",
    )(*parts)


def sum_kernel(keep, got, plain, mirror, stays, stays_other):
    lane = lax.broadcasted_iota(jnp.int32, (ROWS, LANE), 1)
    pad = jnp.zeros((LANE - 2 * ROWS, LANE), F32)
    totals = [keep[pair] + got[pair].astype(F32) for pair in range(2)]
    here = core_here() == 0
    ordered = (jnp.where(here, totals[0], totals[1]), jnp.where(here, totals[1], totals[0]))
    for at, total in enumerate(ordered):
        plain[at] = total[:, :WIDE]
        last = total[:, WIDE:]
        second = jnp.where(lane < 32, pltpu.roll(last, 32, 1), pltpu.roll(total[:, LANE:WIDE], 48, 1))
        turned = jnp.concatenate([last, second, pad], axis=0).T
        mirror[at] = turned[0:ROWS]
        (stays, stays_other)[at][...] = turned[ROWS:2 * ROWS]


def sum_parts(keep, got):
    slim = jax.ShapeDtypeStruct((ROWS, LANE), F32)
    return pl.pallas_call(
        sum_kernel,
        out_shape=(jax.ShapeDtypeStruct((2, ROWS, WIDE), F32), jax.ShapeDtypeStruct((2, ROWS, LANE), F32), slim, slim),
        in_specs=full(2),
        out_specs=tuple(full(4)),
        compiler_params=params(),
        name="sum_parts",
    )(keep, got)


def place_kernel(plain, plain_other, mirror, mirror_other, stays, stays_other, divisor, residual, update):
    row = lax.axis_index("row")
    z, y_lo = lax.div(row, 2), lax.rem(row, 2)
    here = core_here() == 0

    def both(near, far):
        return jnp.where(here, near, far), jnp.where(here, far, near)

    plain_0, plain_1 = both(plain[0], plain_other[...])
    mirror_0, mirror_1 = both(mirror[0], mirror_other[...])
    stays_0, stays_1 = both(stays[...], stays_other[...])

    def piece(array, at):
        return array[:, at * ROWS:(at + 1) * ROWS]

    wide = jnp.concatenate([
        piece(plain_0, 3), piece(plain_1, 4),
        piece(plain_0, 0), piece(mirror_1, 0),
        piece(plain_0, 1), piece(stays_1, 0),
        piece(plain_0, 2), piece(mirror_0, 1),
        piece(plain_0, 4), piece(plain_1, 3),
        piece(mirror_1, 1), piece(plain_1, 2),
        piece(stays_0, 0), piece(plain_1, 1),
        piece(mirror_0, 0), piece(plain_1, 0)], axis=1)
    count = wide.shape[1]
    even = lax.rem(lax.broadcasted_iota(jnp.int32, (1, count), 1), 2 * ROWS) < ROWS
    swapped = jnp.where(even, pltpu.roll(wide, count - ROWS, 1), pltpu.roll(wide, ROWS, 1))
    value = pltpu.roll(jnp.where(y_lo == 0, wide, swapped), z * (2 * ROWS), 1)
    residual[0] = value
    update[0] = value / divisor[...]


def place(*parts):
    out = jax.ShapeDtypeStruct((1, ROWS, 16 * ROWS), F32)
    return pl.pallas_call(
        place_kernel,
        out_shape=(out, out),
        in_specs=full(7),
        out_specs=tuple(full(2)),
        compiler_params=params(),
        name="place",
    )(*parts)


def contraction_weights(amplitudes):
    plain = jnp.swapaxes(amplitudes, 1, 2).reshape(PAIRS, SLAB * SLAB)
    mirror = amplitudes.reshape(PAIRS, SLAB * SLAB)
    both = jnp.concatenate([plain, mirror], axis=0)
    column = np.arange(DEPTH)
    same = np.arange(GROUP)[:, None] == column[None, :] % GROUP
    chunks = []
    for chunk in range(2):
        source = column // (6 * GROUP) * SLAB + 6 * chunk + column // GROUP % 6
        spread = source[None, :] == np.arange(SLAB * SLAB)[:, None]
        wide = jnp.dot(both, jnp.asarray(spread, BF16), preferred_element_type=F32).astype(BF16)
        wide = jnp.where(jnp.asarray(same)[None], wide[:, None, :], jnp.zeros((), BF16))
        chunks.append(wide.reshape(2 * PAIRS * GROUP, DEPTH))
    return chunks


def per_device(factors, amplitudes, vir_energy, pair_energy):
    own = pack_block(factors)
    p1 = shift(own, dz=-1)
    m1 = shift(own, dz=1)
    weights = contraction_weights(amplitudes)
    p2 = shift(p1, dz=-1)
    m2 = shift(m1, dz=1)
    cross = shift(p2, dy=1)
    others = (m1, own, p1, m2, p2)
    raw, divisor = first_star(m2, others, weights, vir_energy, pair_energy)
    keep, send = second_star(cross, others, weights, raw)
    stay, one, two, three = add_cores(keep, shift(send, dc=1))
    keep, send = add_x(stay, shift(two, dx=2), shift(three, dx=-1), shift(one, dx=1))
    plain, mirror, stays, stays_other = sum_parts(keep, shift(send, dh=1))
    stays_other = shift(stays_other, dc=1)
    plain = to_rows(plain, ((-2, 0), (2, 1)))
    mirror = to_rows(mirror, ((-1, 0), (1, 0)))
    plain_other = shift(plain[1], dc=1)
    mirror_other = shift(mirror[1], dc=1)
    return place(plain, plain_other, mirror, mirror_other, stays, stays_other, divisor)


def solution(mesh):
    return jax.shard_map(
        per_device,
        mesh=mesh,
        in_specs=(P("row", None, "col"), P(), P(), P()),
        out_specs=(P("col", "row", None), P("col", "row", None)),
        check_vma=False,
    )
```

```python
import jax
import jax.numpy as jnp
import numpy as np
from jax import lax
from jax.experimental import pallas as pl
from jax.experimental.pallas import tpu as pltpu
from jax.sharding import PartitionSpec as P

ROWS = 48
SLAB = 12
PAIRS = 16
LANE = 128
WIDE = 256
CHUNK = 15
GROUP = 8
GROUPS = ROWS // GROUP
DEPTH = SLAB * SLAB * GROUP
OUT = 3 * LANE
BF16 = jnp.bfloat16
F32 = jnp.float32


def device_of(index):
    row, col = divmod(index, 16)
    return row // 2, row % 2, col // 8, (col // 2) % 4, col % 2


def index_of(z, y_lo, y_hi, x, core):
    return ((z % 8) * 2 + y_lo % 2) * 16 + (y_hi % 2) * 8 + (x % 4) * 2 + core % 2


def shift(array, dz=0, dy=0, dh=0, dx=0, dc=0):
    pairs = []
    for source in range(256):
        z, y, h, x, c = device_of(source)
        pairs.append((source, index_of(z + dz, y + dy, h + dh, x + dx, c + dc)))
    return lax.ppermute(array, ("row", "col"), pairs)


def to_rows(array, flows):
    pairs = []
    for source in range(256):
        z, y, h, x, c = device_of(source)
        dz, dy = flows[c]
        pairs.append((source, index_of(z + dz, y + dy, h, x, c)))
    return lax.ppermute(array, ("row", "col"), pairs)


def full(count):
    return [pl.BlockSpec(memory_space=pltpu.VMEM)] * count


def params():
    return pltpu.CompilerParams(vmem_limit_bytes=24 * 1024 * 1024)


def core_here():
    return lax.rem(lax.axis_index("col"), 2)


def tiles_of(c):
    start, within = CHUNK * (c // 6), c % 6
    return start + 2 * within, start + 2 * within + 1, start + 12 + within % 3, within // 3


def pack_kernel(factors, packed):
    for c in range(SLAB):
        first, second, last, half = tiles_of(c)
        packed[first] = factors[c, :, 0:LANE]
        packed[second] = factors[c, :, LANE:WIDE]
        if half == 0:
            both = [factors[at, :, WIDE:].astype(F32) for at in (c, c + 3)]
            packed[last] = jnp.concatenate(both, axis=1).astype(BF16)


def pack_block(factors):
    return pl.pallas_call(
        pack_kernel,
        out_shape=jax.ShapeDtypeStruct((2 * CHUNK, ROWS, LANE), BF16),
        in_specs=full(1),
        out_specs=full(1)[0],
        compiler_params=params(),
        name="pack",
    )(jnp.transpose(factors, (1, 0, 2)))


def build_left(center, left):
    low = lax.broadcasted_iota(jnp.int32, (ROWS, LANE), 1) < LANE // 2
    zero = jnp.zeros((ROWS, LANE), F32)
    for c in range(SLAB):
        rows = pl.ds(c * ROWS, ROWS)
        main, second, tile, at = tiles_of(c)
        last = center[tile].astype(F32)
        moved = pltpu.roll(last, LANE // 2, 1)
        in_low, in_high = (last, moved) if at == 0 else (moved, last)
        for half in range(2):
            left[half, rows, 0:LANE] = center[main]
            left[half, rows, LANE:2 * LANE] = center[second]
        left[0, rows, 2 * LANE:] = jnp.where(low, in_low, zero).astype(BF16)
        left[1, rows, 2 * LANE:] = jnp.where(low, zero, in_high).astype(BF16)


def build_products(left, near, own, far, m2, p2, products):
    rows = SLAB * GROUP
    for d in range(SLAB):
        columns = []
        first, second, last, half = tiles_of(d)
        for tile in (first, second, last):
            columns.append(jnp.concatenate(
                [near[tile], own[tile], far[tile], m2[tile], p2[tile], far[tile, 32:, :]], axis=0))
        right = jnp.concatenate(columns, axis=1)
        block = lax.dot_general(left[half], right, (((1,), (1,)), ((), ())), preferred_element_type=F32)
        block = block.reshape(SLAB, GROUPS, GROUP, WIDE)
        for g in range(GROUPS):
            part = block[:, g].reshape(rows, WIDE)
            products[g, d * rows:(d + 1) * rows, :] = part.astype(BF16)


def first_kernel(center, m1, own, p1, m2, p2, weights, energy, pair, raw, divisor, left, products):
    shape = divisor.shape
    second = jnp.broadcast_to(energy[...], shape)
    row = lax.axis_index("row") * ROWS + lax.broadcasted_iota(jnp.int32, shape, 0)
    mine = lax.broadcasted_iota(jnp.int32, shape, 1) == row
    first = jnp.sum(jnp.where(mine, second, 0.0), axis=1, keepdims=True)
    divisor[...] = first + second - pair[lax.axis_index("col")]
    build_left(center, left)
    build_products(left, m1, own, p1, m2, p2, products)
    for g in range(GROUPS):
        raw[g] = jnp.dot(weights[...], products[g], preferred_element_type=F32)


def second_kernel(center, m1, own, p1, m2, p2, weights, raw, keep_far, send_far, keep_near, send_near, left, products):
    build_left(center, left)
    build_products(left, p1, own, m1, m2, p2, products)
    half = PAIRS * GROUP
    lane = lax.broadcasted_iota(jnp.int32, (half, LANE), 1)
    wide = lax.broadcasted_iota(jnp.int32, (2, 4, GROUP, LANE), 3)
    inner = (wide >= ROWS) & (wide < 2 * ROWS)
    here = core_here() == 0
    first_half = lax.div(lax.axis_index("col"), 8) == 0
    shape = (2, 4, 2, GROUP, LANE)
    outs = ((keep_far, send_far), (keep_near, send_near))
    for g in range(0, GROUPS, 2):
        held = [[], []]
        for step in range(2):
            mine = jnp.dot(weights[...], products[g + step], preferred_element_type=F32)
            other = raw[g + step]
            for at, inside in enumerate((LANE, 5 * ROWS - LANE, 2 * ROWS)):
                lanes = slice(LANE, WIDE) if at == 1 else slice(0, LANE)
                row = slice(half, 2 * half) if at == 2 else slice(0, half)
                back = slice(half, 2 * half)
                down, up = other[row, lanes], mine[row, lanes]
                if at > 0:
                    down, up = (jnp.where(lane < inside, down, mine[back, lanes]),
                                jnp.where(lane < inside, up, other[back, lanes]))
                down, up = down.reshape(shape), up.reshape(shape)
                if at == 2:
                    down, up = (
                        jnp.stack([down[:, :, 0], jnp.where(inner, up[:, :, 0], down[:, :, 1])], axis=2),
                        jnp.stack([jnp.where(inner, up[:, :, 1], up[:, :, 0]),
                                   jnp.where(inner, down[:, :, 1], up[:, :, 1])], axis=2))
                held[0].append(jnp.where(here, down, up))
                held[1].append(jnp.where(here, up, down))
        rows = pl.ds(g * GROUP, 2 * GROUP)
        for way in range(2):
            for at in range(3):
                lanes = pl.ds(at * LANE, LANE)
                value = jnp.concatenate([held[way][at], held[way][3 + at]], axis=3)
                near = jnp.where(first_half, value[0], value[1])
                far = jnp.where(first_half, value[1], value[0])
                for out, part in ((outs[0][way], far), (outs[1][way], near)):
                    out[:, :, rows, lanes] = part.astype(out.dtype)


def scratch():
    return [
        pltpu.VMEM((2, SLAB * ROWS, 3 * LANE), BF16),
        pltpu.VMEM((GROUPS, DEPTH, WIDE), BF16),
    ]


def first_star(center, others, weights, vir_energy, pair_energy):
    return pl.pallas_call(
        first_kernel,
        out_shape=(jax.ShapeDtypeStruct((GROUPS, 2 * PAIRS * GROUP, WIDE), F32),
                   jax.ShapeDtypeStruct((ROWS, 16 * ROWS), F32)),
        in_specs=full(8) + [pl.BlockSpec(memory_space=pltpu.SMEM)],
        out_specs=tuple(full(2)),
        scratch_shapes=scratch(),
        compiler_params=params(),
        name="first_star",
    )(center, *others, weights, vir_energy[None, :], pair_energy)


def second_star(center, others, weights, raw):
    shape = (4, 2, ROWS, OUT)
    half = (jax.ShapeDtypeStruct(shape, F32), jax.ShapeDtypeStruct(shape, BF16))
    return pl.pallas_call(
        second_kernel,
        out_shape=half + half,
        in_specs=full(8),
        out_specs=tuple(full(4)),
        scratch_shapes=scratch(),
        compiler_params=params(),
        name="second_star",
    )(center, *others, weights, raw)


def core_kernel(keep, got, *outs):
    x = lax.rem(lax.div(lax.axis_index("col"), 2), 4)
    for step, out in enumerate(outs):
        at = lax.rem(x + step, 4)
        out[...] = (keep[at] + got[at].astype(F32)).astype(out.dtype)


def add_cores(keep, got):
    shape = (2, ROWS, OUT)
    return pl.pallas_call(
        core_kernel,
        out_shape=(jax.ShapeDtypeStruct(shape, F32),) + (jax.ShapeDtypeStruct(shape, BF16),) * 3,
        in_specs=full(2),
        out_specs=tuple(full(4)),
        compiler_params=params(),
        name="add_cores",
    )(keep, got)


def x_kernel(stay, two, three, one, send):
    total = stay[...] + one[...].astype(F32) + two[...].astype(F32) + three[...].astype(F32)
    send[...] = total.astype(BF16)


def add_x(*parts):
    return pl.pallas_call(
        x_kernel,
        out_shape=jax.ShapeDtypeStruct((2, ROWS, OUT), BF16),
        in_specs=full(4),
        out_specs=full(1)[0],
        compiler_params=params(),
        name="add_x",
    )(*parts)


def sum_kernel(stay, two, three, one, got, plain, mirror, stays, stays_other):
    lane = lax.broadcasted_iota(jnp.int32, (ROWS, LANE), 1)
    pad = jnp.zeros((LANE - 2 * ROWS, LANE), F32)
    totals = []
    for pair in range(2):
        total = stay[pair]
        for part in (one, two, three, got):
            total = total + part[pair].astype(F32)
        totals.append(total)
    here = core_here() == 0
    ordered = (jnp.where(here, totals[0], totals[1]), jnp.where(here, totals[1], totals[0]))
    for at, total in enumerate(ordered):
        plain[at] = total[:, :WIDE]
        last = total[:, WIDE:]
        second = jnp.where(lane < 32, pltpu.roll(last, 32, 1), pltpu.roll(total[:, LANE:WIDE], 48, 1))
        turned = jnp.concatenate([last, second, pad], axis=0).T
        mirror[at] = turned[0:ROWS]
        (stays, stays_other)[at][...] = turned[ROWS:2 * ROWS]


def sum_parts(*parts):
    slim = jax.ShapeDtypeStruct((ROWS, LANE), F32)
    return pl.pallas_call(
        sum_kernel,
        out_shape=(jax.ShapeDtypeStruct((2, ROWS, WIDE), F32), jax.ShapeDtypeStruct((2, ROWS, LANE), F32), slim, slim),
        in_specs=full(5),
        out_specs=tuple(full(4)),
        compiler_params=params(),
        name="sum_parts",
    )(*parts)


def place_kernel(plain, plain_other, mirror, mirror_other, stays, stays_other, divisor, residual, update):
    row = lax.axis_index("row")
    z, y_lo = lax.div(row, 2), lax.rem(row, 2)
    here = core_here() == 0

    def both(near, far):
        return jnp.where(here, near, far), jnp.where(here, far, near)

    plain_0, plain_1 = both(plain[0], plain_other[...])
    mirror_0, mirror_1 = both(mirror[0], mirror_other[...])
    stays_0, stays_1 = stays[...], stays_other[...]

    def piece(array, at):
        return array[:, at * ROWS:(at + 1) * ROWS]

    wide = jnp.concatenate([
        piece(plain_0, 3), piece(plain_1, 4),
        piece(plain_0, 0), piece(mirror_1, 0),
        piece(plain_0, 1), piece(stays_1, 0),
        piece(plain_0, 2), piece(mirror_0, 1),
        piece(plain_0, 4), piece(plain_1, 3),
        piece(mirror_1, 1), piece(plain_1, 2),
        piece(stays_0, 0), piece(plain_1, 1),
        piece(mirror_0, 0), piece(plain_1, 0)], axis=1)
    count = wide.shape[1]
    even = lax.rem(lax.broadcasted_iota(jnp.int32, (1, count), 1), 2 * ROWS) < ROWS
    swapped = jnp.where(even, pltpu.roll(wide, count - ROWS, 1), pltpu.roll(wide, ROWS, 1))
    value = pltpu.roll(jnp.where(y_lo == 0, wide, swapped), z * (2 * ROWS), 1)
    residual[0] = value
    update[0] = value / divisor[...]


def place(*parts):
    out = jax.ShapeDtypeStruct((1, ROWS, 16 * ROWS), F32)
    return pl.pallas_call(
        place_kernel,
        out_shape=(out, out),
        in_specs=full(7),
        out_specs=tuple(full(2)),
        compiler_params=params(),
        name="place",
    )(*parts)


def contraction_weights(amplitudes):
    plain = jnp.swapaxes(amplitudes, 1, 2).reshape(PAIRS, SLAB * SLAB)
    mirror = amplitudes.reshape(PAIRS, SLAB * SLAB)
    both = jnp.concatenate([plain, mirror], axis=0)
    column = np.arange(DEPTH)
    same = np.arange(GROUP)[:, None] == column[None, :] % GROUP
    spread = column[None, :] // GROUP == np.arange(SLAB * SLAB)[:, None]
    wide = jnp.dot(both, jnp.asarray(spread, BF16), preferred_element_type=F32).astype(BF16)
    wide = jnp.where(jnp.asarray(same)[None], wide[:, None, :], jnp.zeros((), BF16))
    return wide.reshape(2 * PAIRS * GROUP, DEPTH)


def per_device(factors, amplitudes, vir_energy, pair_energy):
    own = pack_block(factors)
    p1 = shift(own, dz=-1)
    m1 = shift(own, dz=1)
    weights = contraction_weights(amplitudes)
    p2 = shift(p1, dz=-1)
    m2 = shift(m1, dz=1)
    cross = shift(p2, dy=1)
    others = (m1, own, p1, m2, p2)
    raw, divisor = first_star(m2, others, weights, vir_energy, pair_energy)
    keep_far, send_far, keep_near, send_near = second_star(cross, others, weights, raw)
    far = add_cores(keep_far, shift(send_far, dc=1))
    near = add_cores(keep_near, shift(send_near, dc=1))

    def along_x(stay, one, two, three):
        return stay, shift(two, dx=2), shift(three, dx=-1), shift(one, dx=1)

    got = shift(add_x(*along_x(*far)), dh=1)
    plain, mirror, stays, stays_other = sum_parts(*along_x(*near), got)
    plain = to_rows(plain, ((-2, 0), (2, 1)))
    mirror = to_rows(mirror, ((-1, 0), (1, 0)))
    plain_other = shift(plain[1], dc=1)
    mirror_other = shift(mirror[1], dc=1)
    return place(plain, plain_other, mirror, mirror_other, stays, stays_other, divisor)


def solution(mesh):
    return jax.shard_map(
        per_device,
        mesh=mesh,
        in_specs=(P("row", None, "col"), P(), P(), P()),
        out_specs=(P("col", "row", None), P("col", "row", None)),
        check_vma=False,
    )
```

```python
import jax
import jax.numpy as jnp
import numpy as np
from jax import lax
from jax.experimental import pallas as pl
from jax.experimental.pallas import tpu as pltpu
from jax.sharding import PartitionSpec as P

ROWS = 48
SLAB = 12
PAIRS = 16
LANE = 128
WIDE = 256
CHUNK = 15
GROUP = 8
GROUPS = ROWS // GROUP
DEPTH = SLAB * SLAB * GROUP
OUT = 3 * LANE
BF16 = jnp.bfloat16
F32 = jnp.float32


def device_of(index):
    row, col = divmod(index, 16)
    return row // 2, row % 2, col // 8, (col // 2) % 4, col % 2


def index_of(z, y_lo, y_hi, x, core):
    return ((z % 8) * 2 + y_lo % 2) * 16 + (y_hi % 2) * 8 + (x % 4) * 2 + core % 2


def shift(array, dz=0, dy=0, dh=0, dx=0, dc=0):
    pairs = []
    for source in range(256):
        z, y, h, x, c = device_of(source)
        pairs.append((source, index_of(z + dz, y + dy, h + dh, x + dx, c + dc)))
    return lax.ppermute(array, ("row", "col"), pairs)


def to_rows(array, flows):
    pairs = []
    for source in range(256):
        z, y, h, x, c = device_of(source)
        dz, dy = flows[c]
        pairs.append((source, index_of(z + dz, y + dy, h, x, c)))
    return lax.ppermute(array, ("row", "col"), pairs)


def full(count):
    return [pl.BlockSpec(memory_space=pltpu.VMEM)] * count


def params():
    return pltpu.CompilerParams(vmem_limit_bytes=24 * 1024 * 1024)


def core_here():
    return lax.rem(lax.axis_index("col"), 2)


def tiles_of(c):
    start, within = CHUNK * (c // 6), c % 6
    return start + 2 * within, start + 2 * within + 1, start + 12 + within % 3, within // 3


def pack_kernel(factors, packed):
    for c in range(SLAB):
        first, second, last, half = tiles_of(c)
        packed[first] = factors[c, :, 0:LANE]
        packed[second] = factors[c, :, LANE:WIDE]
        if half == 0:
            both = [factors[at, :, WIDE:].astype(F32) for at in (c, c + 3)]
            packed[last] = jnp.concatenate(both, axis=1).astype(BF16)


def pack_block(factors):
    return pl.pallas_call(
        pack_kernel,
        out_shape=jax.ShapeDtypeStruct((2 * CHUNK, ROWS, LANE), BF16),
        in_specs=full(1),
        out_specs=full(1)[0],
        compiler_params=params(),
        name="pack",
    )(jnp.transpose(factors, (1, 0, 2)))


def build_left(center, left):
    low = lax.broadcasted_iota(jnp.int32, (ROWS, LANE), 1) < LANE // 2
    zero = jnp.zeros((ROWS, LANE), F32)
    for c in range(SLAB):
        rows = pl.ds(c * ROWS, ROWS)
        main, second, tile, at = tiles_of(c)
        last = center[tile].astype(F32)
        moved = pltpu.roll(last, LANE // 2, 1)
        in_low, in_high = (last, moved) if at == 0 else (moved, last)
        for half in range(2):
            left[half, rows, 0:LANE] = center[main]
            left[half, rows, LANE:2 * LANE] = center[second]
        left[0, rows, 2 * LANE:] = jnp.where(low, in_low, zero).astype(BF16)
        left[1, rows, 2 * LANE:] = jnp.where(low, zero, in_high).astype(BF16)


def build_products(left, near, own, far, m2, p2, products):
    rows = SLAB * GROUP
    for d in range(SLAB):
        columns = []
        first, second, last, half = tiles_of(d)
        for tile in (first, second, last):
            columns.append(jnp.concatenate(
                [near[tile], own[tile], far[tile], m2[tile], p2[tile], far[tile, 32:, :]], axis=0))
        right = jnp.concatenate(columns, axis=1)
        block = lax.dot_general(left[half], right, (((1,), (1,)), ((), ())), preferred_element_type=F32)
        block = block.reshape(SLAB, GROUPS, GROUP, WIDE)
        for g in range(GROUPS):
            part = block[:, g].reshape(rows, WIDE)
            products[g, d * rows:(d + 1) * rows, :] = part.astype(BF16)


def first_kernel(center, m1, own, p1, m2, p2, weights, raw, held, arrived, left, products):
    copy = pltpu.make_async_copy(weights, held, arrived)
    copy.start()
    build_left(center, left)
    build_products(left, m1, own, p1, m2, p2, products)
    copy.wait()
    for g in range(GROUPS):
        raw[g] = jnp.dot(held[...], products[g], preferred_element_type=F32)


def share(weights, products, raw, keep, send, y_hi):
    half = 4 * 2 * GROUP
    lane = lax.broadcasted_iota(jnp.int32, (half, LANE), 1)
    wide = lax.broadcasted_iota(jnp.int32, (4, GROUP, LANE), 2)
    inner = (wide >= ROWS) & (wide < 2 * ROWS)
    here = core_here() == 0
    shape = (4, 2, GROUP, LANE)
    start = pl.multiple_of(y_hi * half, half)
    taken = [pl.ds(start, half), pl.ds(pl.multiple_of(2 * half + start, half), half)]
    chosen = jnp.concatenate([weights[rows, :] for rows in taken], axis=0)
    for g in range(0, GROUPS, 2):
        held = [[], []]
        for step in range(2):
            mine = jnp.dot(chosen, products[g + step], preferred_element_type=F32)
            mine = [mine[:half], mine[half:]]
            other = [raw[g + step, rows, :] for rows in taken]
            for at, inside in enumerate((LANE, 5 * ROWS - LANE, 2 * ROWS)):
                lanes = slice(LANE, WIDE) if at == 1 else slice(0, LANE)
                order = 1 if at == 2 else 0
                down, up = other[order][:, lanes], mine[order][:, lanes]
                if at > 0:
                    down, up = (jnp.where(lane < inside, down, mine[1][:, lanes]),
                                jnp.where(lane < inside, up, other[1][:, lanes]))
                down, up = down.reshape(shape), up.reshape(shape)
                if at == 2:
                    down, up = (
                        jnp.stack([down[:, 0], jnp.where(inner, up[:, 0], down[:, 1])], axis=1),
                        jnp.stack([jnp.where(inner, up[:, 1], up[:, 0]),
                                   jnp.where(inner, down[:, 1], up[:, 1])], axis=1))
                held[0].append(jnp.where(here, down, up))
                held[1].append(jnp.where(here, up, down))
        rows = pl.ds(g * GROUP, 2 * GROUP)
        for out, parts in ((keep, held[0]), (send, held[1])):
            for at in range(3):
                value = jnp.concatenate([parts[at], parts[3 + at]], axis=2)
                out[:, :, rows, at * LANE:(at + 1) * LANE] = value.astype(out.dtype)


def y_hi_here():
    return lax.div(lax.axis_index("col"), 8)


def second_kernel(center, m1, own, p1, m2, p2, weights, raw, keep, send, products, left):
    build_left(center, left)
    build_products(left, p1, own, m1, m2, p2, products)
    share(weights, products, raw, keep, send, 1 - y_hi_here())


def last_kernel(products, weights, raw, keep, send):
    share(weights, products, raw, keep, send, y_hi_here())


def scratch():
    return [
        pltpu.VMEM((2, SLAB * ROWS, 3 * LANE), BF16),
        pltpu.VMEM((GROUPS, DEPTH, WIDE), BF16),
    ]


def weights_scratch():
    return [pltpu.VMEM((2 * PAIRS * GROUP, DEPTH), BF16), pltpu.SemaphoreType.DMA]


def star_cost():
    return pl.CostEstimate(flops=10_000_000_000, bytes_accessed=4_000_000, transcendentals=0)


def first_star(center, others, weights):
    return pl.pallas_call(
        first_kernel,
        out_shape=jax.ShapeDtypeStruct((GROUPS, 2 * PAIRS * GROUP, WIDE), F32),
        in_specs=full(6) + [pl.BlockSpec(memory_space=pl.ANY)],
        out_specs=full(1)[0],
        scratch_shapes=weights_scratch() + scratch(),
        compiler_params=params(),
        cost_estimate=star_cost(),
        name="first_star",
    )(center, *others, weights)


def halves():
    shape = (4, 2, ROWS, OUT)
    return jax.ShapeDtypeStruct(shape, F32), jax.ShapeDtypeStruct(shape, BF16)


def second_star(center, others, weights, raw):
    return pl.pallas_call(
        second_kernel,
        out_shape=halves() + (jax.ShapeDtypeStruct((GROUPS, DEPTH, WIDE), BF16),),
        in_specs=full(8),
        out_specs=tuple(full(3)),
        scratch_shapes=scratch()[:1],
        compiler_params=params(),
        name="second_star",
    )(center, *others, weights, raw)


def last_star(products, weights, raw):
    return pl.pallas_call(
        last_kernel,
        out_shape=halves(),
        in_specs=full(3),
        out_specs=tuple(full(2)),
        compiler_params=params(),
        name="last_star",
    )(products, weights, raw)


def core_kernel(keep, got, *outs):
    x = lax.rem(lax.div(lax.axis_index("col"), 2), 4)
    for step, out in enumerate(outs):
        at = lax.rem(x + step, 4)
        out[...] = (keep[at] + got[at].astype(F32)).astype(out.dtype)


def add_cores(keep, got):
    shape = (2, ROWS, OUT)
    return pl.pallas_call(
        core_kernel,
        out_shape=(jax.ShapeDtypeStruct(shape, F32),) + (jax.ShapeDtypeStruct(shape, BF16),) * 3,
        in_specs=full(2),
        out_specs=tuple(full(4)),
        compiler_params=params(),
        name="add_cores",
    )(keep, got)


def x_kernel(stay, two, three, one, send):
    total = stay[...] + one[...].astype(F32) + two[...].astype(F32) + three[...].astype(F32)
    send[...] = total.astype(BF16)


def add_x(*parts):
    return pl.pallas_call(
        x_kernel,
        out_shape=jax.ShapeDtypeStruct((2, ROWS, OUT), BF16),
        in_specs=full(4),
        out_specs=full(1)[0],
        compiler_params=params(),
        name="add_x",
    )(*parts)


def sum_kernel(stay, two, three, one, got, plain, mirror, stays, stays_other):
    lane = lax.broadcasted_iota(jnp.int32, (ROWS, LANE), 1)
    pad = jnp.zeros((LANE - 2 * ROWS, LANE), F32)
    totals = []
    for pair in range(2):
        total = stay[pair]
        for part in (one, two, three, got):
            total = total + part[pair].astype(F32)
        totals.append(total)
    here = core_here() == 0
    ordered = (jnp.where(here, totals[0], totals[1]), jnp.where(here, totals[1], totals[0]))
    for at, total in enumerate(ordered):
        plain[at] = total[:, :WIDE]
        last = total[:, WIDE:]
        second = jnp.where(lane < 32, pltpu.roll(last, 32, 1), pltpu.roll(total[:, LANE:WIDE], 48, 1))
        turned = jnp.concatenate([last, second, pad], axis=0).T
        mirror[at] = turned[0:ROWS]
        (stays, stays_other)[at][...] = turned[ROWS:2 * ROWS]


def sum_parts(*parts):
    slim = jax.ShapeDtypeStruct((ROWS, LANE), F32)
    return pl.pallas_call(
        sum_kernel,
        out_shape=(jax.ShapeDtypeStruct((2, ROWS, WIDE), F32), jax.ShapeDtypeStruct((2, ROWS, LANE), F32), slim, slim),
        in_specs=full(5),
        out_specs=tuple(full(4)),
        compiler_params=params(),
        name="sum_parts",
    )(*parts)


def place_kernel(plain, plain_other, mirror, mirror_other, stays, stays_other, divisor, residual, update):
    row = lax.axis_index("row")
    z, y_lo = lax.div(row, 2), lax.rem(row, 2)
    here = core_here() == 0

    def both(near, far):
        return jnp.where(here, near, far), jnp.where(here, far, near)

    plain_0, plain_1 = both(plain[0], plain_other[...])
    mirror_0, mirror_1 = both(mirror[0], mirror_other[...])
    stays_0, stays_1 = stays[...], stays_other[...]

    def piece(array, at):
        return array[:, at * ROWS:(at + 1) * ROWS]

    wide = jnp.concatenate([
        piece(plain_0, 3), piece(plain_1, 4),
        piece(plain_0, 0), piece(mirror_1, 0),
        piece(plain_0, 1), piece(stays_1, 0),
        piece(plain_0, 2), piece(mirror_0, 1),
        piece(plain_0, 4), piece(plain_1, 3),
        piece(mirror_1, 1), piece(plain_1, 2),
        piece(stays_0, 0), piece(plain_1, 1),
        piece(mirror_0, 0), piece(plain_1, 0)], axis=1)
    count = wide.shape[1]
    even = lax.rem(lax.broadcasted_iota(jnp.int32, (1, count), 1), 2 * ROWS) < ROWS
    swapped = jnp.where(even, pltpu.roll(wide, count - ROWS, 1), pltpu.roll(wide, ROWS, 1))
    value = pltpu.roll(jnp.where(y_lo == 0, wide, swapped), z * (2 * ROWS), 1)
    residual[0] = value
    update[0] = value / divisor[...]


def place(*parts):
    out = jax.ShapeDtypeStruct((1, ROWS, 16 * ROWS), F32)
    return pl.pallas_call(
        place_kernel,
        out_shape=(out, out),
        in_specs=full(7),
        out_specs=tuple(full(2)),
        compiler_params=params(),
        name="place",
    )(*parts)


def setup_kernel(amplitudes, energy, pair, weights, divisor):
    shape = divisor.shape
    second = jnp.broadcast_to(energy[...].reshape(1, shape[1]), shape)
    row = lax.axis_index("row") * ROWS + lax.broadcasted_iota(jnp.int32, shape, 0)
    mine = lax.broadcasted_iota(jnp.int32, shape, 1) == row
    first = jnp.sum(jnp.where(mine, second, 0.0), axis=1, keepdims=True)
    divisor[...] = first + second - pair[lax.axis_index("col")]
    flat = amplitudes[...].reshape(SLAB * PAIRS, SLAB)
    column = lax.broadcasted_iota(jnp.int32, (1, DEPTH), 1)
    slab = lax.broadcasted_iota(jnp.int32, (SLAB, DEPTH), 0)
    within = lax.broadcasted_iota(jnp.int32, (PAIRS * GROUP, DEPTH), 0)
    same = lax.rem(within, GROUP) == lax.rem(column, GROUP)
    d, c = lax.div(column, SLAB * GROUP), lax.rem(lax.div(column, GROUP), SLAB)
    for order, (outer, inner) in enumerate(((c, d), (d, c))):
        spread = jnp.where(slab == inner, 1.0, 0.0).astype(BF16)
        wide = jnp.dot(flat, spread, preferred_element_type=F32).reshape(SLAB, PAIRS, DEPTH)
        total = jnp.where(outer == 0, wide[0], 0.0)
        for at in range(1, SLAB):
            total = jnp.where(outer == at, wide[at], total)
        total = jnp.broadcast_to(total[:, None, :], (PAIRS, GROUP, DEPTH)).reshape(PAIRS * GROUP, DEPTH)
        weights[order * PAIRS * GROUP:(order + 1) * PAIRS * GROUP, :] = jnp.where(same, total, 0.0).astype(BF16)


def setup(amplitudes, vir_energy, pair_energy):
    return pl.pallas_call(
        setup_kernel,
        out_shape=(jax.ShapeDtypeStruct((2 * PAIRS * GROUP, DEPTH), BF16), jax.ShapeDtypeStruct((ROWS, 16 * ROWS), F32)),
        in_specs=full(2) + [pl.BlockSpec(memory_space=pltpu.SMEM)],
        out_specs=tuple(full(2)),
        compiler_params=params(),
        name="setup",
    )(jnp.transpose(amplitudes, (1, 0, 2)), vir_energy, pair_energy)


def per_device(factors, amplitudes, vir_energy, pair_energy):
    own = pack_block(factors)
    p1 = shift(own, dz=-1)
    m1 = shift(own, dz=1)
    weights, divisor = setup(amplitudes, vir_energy, pair_energy)
    p2 = shift(p1, dz=-1)
    m2 = shift(m1, dz=1)
    cross = shift(p2, dy=1)
    others = (m1, own, p1, m2, p2)
    raw = first_star(m2, others, weights)
    keep, send, products = second_star(cross, others, weights, raw)
    far = add_cores(keep, shift(send, dc=1))
    keep, send = last_star(products, weights, raw)
    near = add_cores(keep, shift(send, dc=1))

    def along_x(stay, one, two, three):
        return stay, shift(two, dx=2), shift(three, dx=-1), shift(one, dx=1)

    got = shift(add_x(*along_x(*far)), dh=1)
    plain, mirror, stays, stays_other = sum_parts(*along_x(*near), got)
    plain = to_rows(plain, ((-2, 0), (2, 1)))
    mirror = to_rows(mirror, ((-1, 0), (1, 0)))
    plain_other = shift(plain[1], dc=1)
    mirror_other = shift(mirror[1], dc=1)
    return place(plain, plain_other, mirror, mirror_other, stays, stays_other, divisor)


def solution(mesh):
    return jax.shard_map(
        per_device,
        mesh=mesh,
        in_specs=(P("row", None, "col"), P(), P(), P()),
        out_specs=(P("col", "row", None), P("col", "row", None)),
        check_vma=False,
    )
```

```python
import jax
import jax.numpy as jnp
import numpy as np
from jax import lax
from jax.experimental import pallas as pl
from jax.experimental.pallas import tpu as pltpu
from jax.sharding import PartitionSpec as P

ROWS = 48
SLAB = 12
PAIRS = 16
LANE = 128
WIDE = 256
CHUNK = 15
GROUP = 8
GROUPS = ROWS // GROUP
DEPTH = SLAB * SLAB * GROUP
OUT = 3 * LANE
BF16 = jnp.bfloat16
F32 = jnp.float32


def device_of(index):
    row, col = divmod(index, 16)
    return row // 2, row % 2, col // 8, (col // 2) % 4, col % 2


def index_of(z, y_lo, y_hi, x, core):
    return ((z % 8) * 2 + y_lo % 2) * 16 + (y_hi % 2) * 8 + (x % 4) * 2 + core % 2


def shift(array, dz=0, dy=0, dh=0, dx=0, dc=0):
    pairs = []
    for source in range(256):
        z, y, h, x, c = device_of(source)
        pairs.append((source, index_of(z + dz, y + dy, h + dh, x + dx, c + dc)))
    return lax.ppermute(array, ("row", "col"), pairs)


def to_rows(array, flows):
    pairs = []
    for source in range(256):
        z, y, h, x, c = device_of(source)
        dz, dy = flows[c]
        pairs.append((source, index_of(z + dz, y + dy, h, x, c)))
    return lax.ppermute(array, ("row", "col"), pairs)


def full(count):
    return [pl.BlockSpec(memory_space=pltpu.VMEM)] * count


def params():
    return pltpu.CompilerParams(vmem_limit_bytes=24 * 1024 * 1024)


def core_here():
    return lax.rem(lax.axis_index("col"), 2)


class Halves:
    def __init__(self, one, two):
        self.parts = one, two

    def __getitem__(self, at):
        tile, rest = (at[0], at[1:]) if isinstance(at, tuple) else (at, ())
        return self.parts[tile // CHUNK][(tile % CHUNK, *rest)]

    def __setitem__(self, tile, value):
        self.parts[tile // CHUNK][tile % CHUNK] = value


def tiles_of(c):
    start, within = CHUNK * (c // 6), c % 6
    return start + 2 * within, start + 2 * within + 1, start + 12 + within % 3, within // 3


def pack_kernel(factors, one, two):
    packed = Halves(one, two)
    for c in range(SLAB):
        first, second, last, half = tiles_of(c)
        packed[first] = factors[c, :, 0:LANE]
        packed[second] = factors[c, :, LANE:WIDE]
        if half == 0:
            both = [factors[at, :, WIDE:].astype(F32) for at in (c, c + 3)]
            packed[last] = jnp.concatenate(both, axis=1).astype(BF16)


def pack_block(factors):
    return pl.pallas_call(
        pack_kernel,
        out_shape=(jax.ShapeDtypeStruct((CHUNK, ROWS, LANE), BF16),) * 2,
        in_specs=full(1),
        out_specs=tuple(full(2)),
        compiler_params=params(),
        name="pack",
    )(jnp.transpose(factors, (1, 0, 2)))


def build_left(center, left):
    low = lax.broadcasted_iota(jnp.int32, (ROWS, LANE), 1) < LANE // 2
    zero = jnp.zeros((ROWS, LANE), F32)
    for c in range(SLAB):
        rows = pl.ds(c * ROWS, ROWS)
        main, second, tile, at = tiles_of(c)
        last = center[tile].astype(F32)
        moved = pltpu.roll(last, LANE // 2, 1)
        in_low, in_high = (last, moved) if at == 0 else (moved, last)
        for half in range(2):
            left[half, rows, 0:LANE] = center[main]
            left[half, rows, LANE:2 * LANE] = center[second]
        left[0, rows, 2 * LANE:] = jnp.where(low, in_low, zero).astype(BF16)
        left[1, rows, 2 * LANE:] = jnp.where(low, zero, in_high).astype(BF16)


def build_products(left, near, own, far, m2, p2, products):
    rows = SLAB * GROUP
    for d in range(SLAB):
        columns = []
        first, second, last, half = tiles_of(d)
        for tile in (first, second, last):
            columns.append(jnp.concatenate(
                [near[tile], own[tile], far[tile], m2[tile], p2[tile], far[tile, 32:, :]], axis=0))
        right = jnp.concatenate(columns, axis=1)
        block = lax.dot_general(left[half], right, (((1,), (1,)), ((), ())), preferred_element_type=F32)
        block = block.reshape(SLAB, GROUPS, GROUP, WIDE)
        for g in range(GROUPS):
            part = block[:, g].reshape(rows, WIDE)
            products[g, d * rows:(d + 1) * rows, :] = part.astype(BF16)


def paired(refs):
    return [Halves(refs[at], refs[at + 1]) for at in range(0, len(refs), 2)]


def first_kernel(*refs):
    m1, own, p1, m2, p2 = paired(refs[:10])
    weights, raw, held, arrived, left, products = refs[10:]
    copy = pltpu.make_async_copy(weights, held, arrived)
    copy.start()
    build_left(m2, left)
    build_products(left, m1, own, p1, m2, p2, products)
    copy.wait()
    for g in range(GROUPS):
        raw[g] = jnp.dot(held[...], products[g], preferred_element_type=F32)


def share(weights, products, raw, keep, send, y_hi):
    half = 4 * 2 * GROUP
    lane = lax.broadcasted_iota(jnp.int32, (half, LANE), 1)
    wide = lax.broadcasted_iota(jnp.int32, (4, GROUP, LANE), 2)
    inner = (wide >= ROWS) & (wide < 2 * ROWS)
    here = core_here() == 0
    shape = (4, 2, GROUP, LANE)
    start = pl.multiple_of(y_hi * half, half)
    taken = [pl.ds(start, half), pl.ds(pl.multiple_of(2 * half + start, half), half)]
    chosen = jnp.concatenate([weights[rows, :] for rows in taken], axis=0)
    for g in range(0, GROUPS, 2):
        held = [[], []]
        for step in range(2):
            mine = jnp.dot(chosen, products[g + step], preferred_element_type=F32)
            mine = [mine[:half], mine[half:]]
            other = [raw[g + step, rows, :] for rows in taken]
            for at, inside in enumerate((LANE, 5 * ROWS - LANE, 2 * ROWS)):
                lanes = slice(LANE, WIDE) if at == 1 else slice(0, LANE)
                order = 1 if at == 2 else 0
                down, up = other[order][:, lanes], mine[order][:, lanes]
                if at > 0:
                    down, up = (jnp.where(lane < inside, down, mine[1][:, lanes]),
                                jnp.where(lane < inside, up, other[1][:, lanes]))
                down, up = down.reshape(shape), up.reshape(shape)
                if at == 2:
                    down, up = (
                        jnp.stack([down[:, 0], jnp.where(inner, up[:, 0], down[:, 1])], axis=1),
                        jnp.stack([jnp.where(inner, up[:, 1], up[:, 0]),
                                   jnp.where(inner, down[:, 1], up[:, 1])], axis=1))
                held[0].append(jnp.where(here, down, up))
                held[1].append(jnp.where(here, up, down))
        rows = pl.ds(g * GROUP, 2 * GROUP)
        for out, parts in ((keep, held[0]), (send, held[1])):
            for at in range(3):
                value = jnp.concatenate([parts[at], parts[3 + at]], axis=2)
                out[:, :, rows, at * LANE:(at + 1) * LANE] = value.astype(out.dtype)


def y_hi_here():
    return lax.div(lax.axis_index("col"), 8)


def second_kernel(*refs):
    center, m1, own, p1, m2, p2 = paired(refs[:12])
    weights, raw, keep, send, products, left = refs[12:]
    build_left(center, left)
    build_products(left, p1, own, m1, m2, p2, products)
    share(weights, products, raw, keep, send, 1 - y_hi_here())


def last_kernel(products, weights, raw, vir_energy, pair_energy, keep, send, divisor, energy, pair, arrived):
    copies = (pltpu.make_async_copy(vir_energy, energy, arrived.at[0]),
              pltpu.make_async_copy(pair_energy, pair, arrived.at[1]))
    for copy in copies:
        copy.start()
    share(weights, products, raw, keep, send, y_hi_here())
    for copy in copies:
        copy.wait()
    shape = divisor.shape
    second = jnp.broadcast_to(energy[...].reshape(1, shape[1]), shape)
    row = lax.axis_index("row") * ROWS + lax.broadcasted_iota(jnp.int32, shape, 0)
    mine = lax.broadcasted_iota(jnp.int32, shape, 1) == row
    first = jnp.sum(jnp.where(mine, second, 0.0), axis=1, keepdims=True)
    divisor[...] = first + second - pair[lax.axis_index("col")]


def scratch():
    return [
        pltpu.VMEM((2, SLAB * ROWS, 3 * LANE), BF16),
        pltpu.VMEM((GROUPS, DEPTH, WIDE), BF16),
    ]


def weights_scratch():
    return [pltpu.VMEM((2 * PAIRS * GROUP, DEPTH), BF16), pltpu.SemaphoreType.DMA]


def star_cost():
    return pl.CostEstimate(flops=10_000_000_000, bytes_accessed=4_000_000, transcendentals=0)


def first_star(others, weights):
    return pl.pallas_call(
        first_kernel,
        out_shape=jax.ShapeDtypeStruct((GROUPS, 2 * PAIRS * GROUP, WIDE), F32),
        in_specs=full(10) + [pl.BlockSpec(memory_space=pl.ANY)],
        out_specs=full(1)[0],
        scratch_shapes=weights_scratch() + scratch(),
        compiler_params=params(),
        cost_estimate=star_cost(),
        name="first_star",
    )(*others, weights)


def halves():
    shape = (4, 2, ROWS, OUT)
    return jax.ShapeDtypeStruct(shape, F32), jax.ShapeDtypeStruct(shape, BF16)


def second_star(center, others, weights, raw):
    return pl.pallas_call(
        second_kernel,
        out_shape=halves() + (jax.ShapeDtypeStruct((GROUPS, DEPTH, WIDE), BF16),),
        in_specs=full(14),
        out_specs=tuple(full(3)),
        scratch_shapes=scratch()[:1],
        compiler_params=params(),
        name="second_star",
    )(*center, *others, weights, raw)


def last_star(products, weights, raw, vir_energy, pair_energy):
    return pl.pallas_call(
        last_kernel,
        out_shape=halves() + (jax.ShapeDtypeStruct((ROWS, 16 * ROWS), F32),),
        in_specs=full(3) + [pl.BlockSpec(memory_space=pl.ANY)] * 2,
        out_specs=tuple(full(3)),
        scratch_shapes=[
            pltpu.VMEM(vir_energy.shape, F32),
            pltpu.SMEM(pair_energy.shape, F32),
            pltpu.SemaphoreType.DMA((2,)),
        ],
        compiler_params=params(),
        name="last_star",
    )(products, weights, raw, vir_energy, pair_energy)


def core_kernel(keep, got, *outs):
    x = lax.rem(lax.div(lax.axis_index("col"), 2), 4)
    for step, out in enumerate(outs):
        at = lax.rem(x + step, 4)
        out[...] = (keep[at] + got[at].astype(F32)).astype(out.dtype)


def add_cores(keep, got):
    shape = (2, ROWS, OUT)
    return pl.pallas_call(
        core_kernel,
        out_shape=(jax.ShapeDtypeStruct(shape, F32),) + (jax.ShapeDtypeStruct(shape, BF16),) * 3,
        in_specs=full(2),
        out_specs=tuple(full(4)),
        compiler_params=params(),
        name="add_cores",
    )(keep, got)


def x_kernel(stay, two, three, one, send):
    total = stay[...] + one[...].astype(F32) + two[...].astype(F32) + three[...].astype(F32)
    send[...] = total.astype(BF16)


def add_x(*parts):
    return pl.pallas_call(
        x_kernel,
        out_shape=jax.ShapeDtypeStruct((2, ROWS, OUT), BF16),
        in_specs=full(4),
        out_specs=full(1)[0],
        compiler_params=params(),
        name="add_x",
    )(*parts)


def sum_kernel(stay, two, three, one, got, plain, mirror, stays, stays_other):
    lane = lax.broadcasted_iota(jnp.int32, (ROWS, LANE), 1)
    pad = jnp.zeros((LANE - 2 * ROWS, LANE), F32)
    totals = []
    for pair in range(2):
        total = stay[pair]
        for part in (one, two, three, got):
            total = total + part[pair].astype(F32)
        totals.append(total)
    here = core_here() == 0
    ordered = (jnp.where(here, totals[0], totals[1]), jnp.where(here, totals[1], totals[0]))
    for at, total in enumerate(ordered):
        plain[at] = total[:, :WIDE]
        last = total[:, WIDE:]
        second = jnp.where(lane < 32, pltpu.roll(last, 32, 1), pltpu.roll(total[:, LANE:WIDE], 48, 1))
        turned = jnp.concatenate([last, second, pad], axis=0).T
        mirror[at] = turned[0:ROWS]
        (stays, stays_other)[at][...] = turned[ROWS:2 * ROWS]


def sum_parts(*parts):
    slim = jax.ShapeDtypeStruct((ROWS, LANE), F32)
    return pl.pallas_call(
        sum_kernel,
        out_shape=(jax.ShapeDtypeStruct((2, ROWS, WIDE), F32), jax.ShapeDtypeStruct((2, ROWS, LANE), F32), slim, slim),
        in_specs=full(5),
        out_specs=tuple(full(4)),
        compiler_params=params(),
        name="sum_parts",
    )(*parts)


def place_kernel(plain, plain_other, mirror, mirror_other, stays, stays_other, divisor, residual, update):
    row = lax.axis_index("row")
    z, y_lo = lax.div(row, 2), lax.rem(row, 2)
    here = core_here() == 0

    def both(near, far):
        return jnp.where(here, near, far), jnp.where(here, far, near)

    plain_0, plain_1 = both(plain[0], plain_other[...])
    mirror_0, mirror_1 = both(mirror[0], mirror_other[...])
    stays_0, stays_1 = stays[...], stays_other[...]

    def piece(array, at):
        return array[:, at * ROWS:(at + 1) * ROWS]

    wide = jnp.concatenate([
        piece(plain_0, 3), piece(plain_1, 4),
        piece(plain_0, 0), piece(mirror_1, 0),
        piece(plain_0, 1), piece(stays_1, 0),
        piece(plain_0, 2), piece(mirror_0, 1),
        piece(plain_0, 4), piece(plain_1, 3),
        piece(mirror_1, 1), piece(plain_1, 2),
        piece(stays_0, 0), piece(plain_1, 1),
        piece(mirror_0, 0), piece(plain_1, 0)], axis=1)
    count = wide.shape[1]
    even = lax.rem(lax.broadcasted_iota(jnp.int32, (1, count), 1), 2 * ROWS) < ROWS
    swapped = jnp.where(even, pltpu.roll(wide, count - ROWS, 1), pltpu.roll(wide, ROWS, 1))
    value = pltpu.roll(jnp.where(y_lo == 0, wide, swapped), z * (2 * ROWS), 1)
    residual[0] = value
    update[0] = value / divisor[...]


def place(*parts):
    out = jax.ShapeDtypeStruct((1, ROWS, 16 * ROWS), F32)
    return pl.pallas_call(
        place_kernel,
        out_shape=(out, out),
        in_specs=full(7),
        out_specs=tuple(full(2)),
        compiler_params=params(),
        name="place",
    )(*parts)


def weights_kernel(amplitudes, weights, held, arrived):
    copy = pltpu.make_async_copy(amplitudes, held, arrived)
    copy.start()
    column = lax.broadcasted_iota(jnp.int32, (1, DEPTH), 1)
    slab = lax.broadcasted_iota(jnp.int32, (SLAB, DEPTH), 0)
    within = lax.broadcasted_iota(jnp.int32, (PAIRS * GROUP, DEPTH), 0)
    same = lax.rem(within, GROUP) == lax.rem(column, GROUP)
    d, c = lax.div(column, SLAB * GROUP), lax.rem(lax.div(column, GROUP), SLAB)
    copy.wait()
    flat = held[...].reshape(SLAB * PAIRS, SLAB)
    for order, (outer, inner) in enumerate(((c, d), (d, c))):
        spread = jnp.where(slab == inner, 1.0, 0.0).astype(BF16)
        wide = jnp.dot(flat, spread, preferred_element_type=F32).reshape(SLAB, PAIRS, DEPTH)
        total = jnp.where(outer == 0, wide[0], 0.0)
        for at in range(1, SLAB):
            total = jnp.where(outer == at, wide[at], total)
        total = jnp.broadcast_to(total[:, None, :], (PAIRS, GROUP, DEPTH)).reshape(PAIRS * GROUP, DEPTH)
        weights[order * PAIRS * GROUP:(order + 1) * PAIRS * GROUP, :] = jnp.where(same, total, 0.0).astype(BF16)


def contraction_weights(amplitudes):
    return pl.pallas_call(
        weights_kernel,
        out_shape=jax.ShapeDtypeStruct((2 * PAIRS * GROUP, DEPTH), BF16),
        in_specs=[pl.BlockSpec(memory_space=pl.ANY)],
        out_specs=full(1)[0],
        scratch_shapes=[pltpu.VMEM((SLAB, PAIRS, SLAB), BF16), pltpu.SemaphoreType.DMA],
        compiler_params=params(),
        name="weights",
    )(jnp.transpose(amplitudes, (1, 0, 2)))


def per_device(factors, amplitudes, vir_energy, pair_energy):
    def moved(block, **by):
        return [shift(part, **by) for part in block]

    own = pack_block(factors)
    p1 = moved(own, dz=-1)
    m1 = moved(own, dz=1)
    weights = contraction_weights(amplitudes)
    p2 = moved(p1, dz=-1)
    m2 = moved(m1, dz=1)
    cross = moved(p2, dy=1)
    others = (*m1, *own, *p1, *m2, *p2)
    raw = first_star(others, weights)
    keep, send, products = second_star(cross, others, weights, raw)
    far = add_cores(keep, shift(send, dc=1))
    keep, send, divisor = last_star(products, weights, raw, vir_energy, pair_energy)
    near = add_cores(keep, shift(send, dc=1))

    def along_x(stay, one, two, three):
        return stay, shift(two, dx=2), shift(three, dx=-1), shift(one, dx=1)

    got = shift(add_x(*along_x(*far)), dh=1)
    plain, mirror, stays, stays_other = sum_parts(*along_x(*near), got)
    plain = to_rows(plain, ((-2, 0), (2, 1)))
    mirror = to_rows(mirror, ((-1, 0), (1, 0)))
    plain_other = shift(plain[1], dc=1)
    mirror_other = shift(mirror[1], dc=1)
    return place(plain, plain_other, mirror, mirror_other, stays, stays_other, divisor)


def solution(mesh):
    return jax.shard_map(
        per_device,
        mesh=mesh,
        in_specs=(P("row", None, "col"), P(), P(), P()),
        out_specs=(P("col", "row", None), P("col", "row", None)),
        check_vma=False,
    )
```

```python
import jax
import jax.numpy as jnp
import numpy as np
from jax import lax
from jax.experimental import pallas as pl
from jax.experimental.pallas import tpu as pltpu
from jax.sharding import PartitionSpec as P

ROWS = 48
SLAB = 12
PAIRS = 16
LANE = 128
WIDE = 256
CHUNK = 15
GROUP = 8
GROUPS = ROWS // GROUP
DEPTH = SLAB * SLAB * GROUP
OUT = 3 * LANE
BF16 = jnp.bfloat16
F32 = jnp.float32


def device_of(index):
    row, col = divmod(index, 16)
    return row // 2, row % 2, col // 8, (col // 2) % 4, col % 2


def index_of(z, y_lo, y_hi, x, core):
    return ((z % 8) * 2 + y_lo % 2) * 16 + (y_hi % 2) * 8 + (x % 4) * 2 + core % 2


def shift(array, dz=0, dy=0, dh=0, dx=0, dc=0):
    pairs = []
    for source in range(256):
        z, y, h, x, c = device_of(source)
        pairs.append((source, index_of(z + dz, y + dy, h + dh, x + dx, c + dc)))
    return lax.ppermute(array, ("row", "col"), pairs)


def to_rows(array, flows):
    pairs = []
    for source in range(256):
        z, y, h, x, c = device_of(source)
        dz, dy = flows[c]
        pairs.append((source, index_of(z + dz, y + dy, h, x, c)))
    return lax.ppermute(array, ("row", "col"), pairs)


def full(count):
    return [pl.BlockSpec(memory_space=pltpu.VMEM)] * count


def params():
    return pltpu.CompilerParams(vmem_limit_bytes=24 * 1024 * 1024)


def core_here():
    return lax.rem(lax.axis_index("col"), 2)


class Halves:
    def __init__(self, one, two):
        self.parts = one, two

    def __getitem__(self, at):
        tile, rest = (at[0], at[1:]) if isinstance(at, tuple) else (at, ())
        return self.parts[tile // CHUNK][(tile % CHUNK, *rest)]

    def __setitem__(self, tile, value):
        self.parts[tile // CHUNK][tile % CHUNK] = value


def tiles_of(c):
    start, within = CHUNK * (c // 6), c % 6
    return start + 2 * within, start + 2 * within + 1, start + 12 + within % 3, within // 3


def pack_kernel(factors, one, two):
    packed = Halves(one, two)
    for c in range(SLAB):
        first, second, last, half = tiles_of(c)
        packed[first] = factors[c, :, 0:LANE]
        packed[second] = factors[c, :, LANE:WIDE]
        if half == 0:
            both = [factors[at, :, WIDE:].astype(F32) for at in (c, c + 3)]
            packed[last] = jnp.concatenate(both, axis=1).astype(BF16)


def pack_block(factors):
    return pl.pallas_call(
        pack_kernel,
        out_shape=(jax.ShapeDtypeStruct((CHUNK, ROWS, LANE), BF16),) * 2,
        in_specs=full(1),
        out_specs=tuple(full(2)),
        compiler_params=params(),
        name="pack",
    )(jnp.transpose(factors, (1, 0, 2)))


def build_left(center, left):
    low = lax.broadcasted_iota(jnp.int32, (ROWS, LANE), 1) < LANE // 2
    zero = jnp.zeros((ROWS, LANE), F32)
    for c in range(SLAB):
        rows = pl.ds(c * ROWS, ROWS)
        main, second, tile, at = tiles_of(c)
        last = center[tile].astype(F32)
        moved = pltpu.roll(last, LANE // 2, 1)
        in_low, in_high = (last, moved) if at == 0 else (moved, last)
        for half in range(2):
            left[half, rows, 0:LANE] = center[main]
            left[half, rows, LANE:2 * LANE] = center[second]
        left[0, rows, 2 * LANE:] = jnp.where(low, in_low, zero).astype(BF16)
        left[1, rows, 2 * LANE:] = jnp.where(low, zero, in_high).astype(BF16)


def build_products(left, near, own, far, m2, p2, products):
    rows = SLAB * GROUP
    for d in range(SLAB):
        columns = []
        first, second, last, half = tiles_of(d)
        for tile in (first, second, last):
            columns.append(jnp.concatenate(
                [near[tile], own[tile], far[tile], m2[tile], p2[tile], far[tile, 32:, :]], axis=0))
        right = jnp.concatenate(columns, axis=1)
        block = lax.dot_general(left[half], right, (((1,), (1,)), ((), ())), preferred_element_type=F32)
        block = block.reshape(SLAB, GROUPS, GROUP, WIDE)
        for g in range(GROUPS):
            part = block[:, g].reshape(rows, WIDE)
            products[g, d * rows:(d + 1) * rows, :] = part.astype(BF16)


def paired(refs):
    return [Halves(refs[at], refs[at + 1]) for at in range(0, len(refs), 2)]


def first_kernel(*refs):
    m1, own, p1, m2, p2 = paired(refs[:10])
    weights, raw, held, arrived, left, products = refs[10:]
    copy = pltpu.make_async_copy(weights, held, arrived)
    copy.start()
    build_left(m2, left)
    build_products(left, m1, own, p1, m2, p2, products)
    copy.wait()
    for g in range(GROUPS):
        raw[g] = jnp.dot(held[...], products[g], preferred_element_type=F32)


def share(weights, products, raw, keep, send, y_hi):
    half = 4 * 2 * GROUP
    lane = lax.broadcasted_iota(jnp.int32, (half, LANE), 1)
    wide = lax.broadcasted_iota(jnp.int32, (4, GROUP, LANE), 2)
    inner = (wide >= ROWS) & (wide < 2 * ROWS)
    here = core_here() == 0
    shape = (4, 2, GROUP, LANE)
    start = pl.multiple_of(y_hi * half, half)
    taken = [pl.ds(start, half), pl.ds(pl.multiple_of(2 * half + start, half), half)]
    chosen = jnp.concatenate([weights[rows, :] for rows in taken], axis=0)
    for g in range(0, GROUPS, 2):
        held = [[], []]
        for step in range(2):
            mine = jnp.dot(chosen, products[g + step], preferred_element_type=F32)
            mine = [mine[:half], mine[half:]]
            other = [raw[g + step, rows, :] for rows in taken]
            for at, inside in enumerate((LANE, 5 * ROWS - LANE, 2 * ROWS)):
                lanes = slice(LANE, WIDE) if at == 1 else slice(0, LANE)
                order = 1 if at == 2 else 0
                down, up = other[order][:, lanes], mine[order][:, lanes]
                if at > 0:
                    down, up = (jnp.where(lane < inside, down, mine[1][:, lanes]),
                                jnp.where(lane < inside, up, other[1][:, lanes]))
                down, up = down.reshape(shape), up.reshape(shape)
                if at == 2:
                    down, up = (
                        jnp.stack([down[:, 0], jnp.where(inner, up[:, 0], down[:, 1])], axis=1),
                        jnp.stack([jnp.where(inner, up[:, 1], up[:, 0]),
                                   jnp.where(inner, down[:, 1], up[:, 1])], axis=1))
                held[0].append(jnp.where(here, down, up))
                held[1].append(jnp.where(here, up, down))
        rows = pl.ds(g * GROUP, 2 * GROUP)
        for out, parts in ((keep, held[0]), (send, held[1])):
            for at in range(3):
                value = jnp.concatenate([parts[at], parts[3 + at]], axis=2)
                out[:, :, rows, at * LANE:(at + 1) * LANE] = value.astype(out.dtype)


def y_hi_here():
    return lax.div(lax.axis_index("col"), 8)


def second_kernel(*refs):
    center, m1, own, p1, m2, p2 = paired(refs[:12])
    weights, raw, keep, send, products, left = refs[12:]
    build_left(center, left)
    build_products(left, p1, own, m1, m2, p2, products)
    share(weights, products, raw, keep, send, 1 - y_hi_here())


def last_kernel(products, weights, raw, vir_energy, pair_energy, keep, send, divisor, energy, pair, arrived):
    copies = (pltpu.make_async_copy(vir_energy, energy, arrived.at[0]),
              pltpu.make_async_copy(pair_energy, pair, arrived.at[1]))
    for copy in copies:
        copy.start()
    share(weights, products, raw, keep, send, y_hi_here())
    for copy in copies:
        copy.wait()
    shape = divisor.shape
    second = jnp.broadcast_to(energy[...].reshape(1, shape[1]), shape)
    row = lax.axis_index("row") * ROWS + lax.broadcasted_iota(jnp.int32, shape, 0)
    mine = lax.broadcasted_iota(jnp.int32, shape, 1) == row
    first = jnp.sum(jnp.where(mine, second, 0.0), axis=1, keepdims=True)
    divisor[...] = first + second - pair[lax.axis_index("col")]


def scratch():
    return [
        pltpu.VMEM((2, SLAB * ROWS, 3 * LANE), BF16),
        pltpu.VMEM((GROUPS, DEPTH, WIDE), BF16),
    ]


def weights_scratch():
    return [pltpu.VMEM((2 * PAIRS * GROUP, DEPTH), BF16), pltpu.SemaphoreType.DMA]


def star_cost():
    return pl.CostEstimate(flops=10_000_000_000, bytes_accessed=4_000_000, transcendentals=0)


def first_star(others, weights):
    return pl.pallas_call(
        first_kernel,
        out_shape=jax.ShapeDtypeStruct((GROUPS, 2 * PAIRS * GROUP, WIDE), F32),
        in_specs=full(10) + [pl.BlockSpec(memory_space=pl.ANY)],
        out_specs=full(1)[0],
        scratch_shapes=weights_scratch() + scratch(),
        compiler_params=params(),
        cost_estimate=star_cost(),
        name="first_star",
    )(*others, weights)


def halves():
    shape = (4, 2, ROWS, OUT)
    return jax.ShapeDtypeStruct(shape, F32), jax.ShapeDtypeStruct(shape, BF16)


def second_star(center, others, weights, raw):
    return pl.pallas_call(
        second_kernel,
        out_shape=halves() + (jax.ShapeDtypeStruct((GROUPS, DEPTH, WIDE), BF16),),
        in_specs=full(14),
        out_specs=tuple(full(3)),
        scratch_shapes=scratch()[:1],
        compiler_params=params(),
        name="second_star",
    )(*center, *others, weights, raw)


def last_star(products, weights, raw, vir_energy, pair_energy):
    return pl.pallas_call(
        last_kernel,
        out_shape=halves() + (jax.ShapeDtypeStruct((ROWS, 16 * ROWS), F32),),
        in_specs=full(3) + [pl.BlockSpec(memory_space=pl.ANY)] * 2,
        out_specs=tuple(full(3)),
        scratch_shapes=[
            pltpu.VMEM(vir_energy.shape, F32),
            pltpu.SMEM(pair_energy.shape, F32),
            pltpu.SemaphoreType.DMA((2,)),
        ],
        compiler_params=params(),
        name="last_star",
    )(products, weights, raw, vir_energy, pair_energy)


def core_kernel(keep, got, *outs):
    x = lax.rem(lax.div(lax.axis_index("col"), 2), 4)
    for step, out in enumerate(outs):
        at = lax.rem(x + step, 4)
        out[...] = (keep[at] + got[at].astype(F32)).astype(out.dtype)


def add_cores(keep, got):
    shape = (2, ROWS, OUT)
    return pl.pallas_call(
        core_kernel,
        out_shape=(jax.ShapeDtypeStruct(shape, F32),) + (jax.ShapeDtypeStruct(shape, BF16),) * 3,
        in_specs=full(2),
        out_specs=tuple(full(4)),
        compiler_params=params(),
        name="add_cores",
    )(keep, got)


def x_kernel(stay, two, three, one, send):
    total = stay[...] + one[...].astype(F32) + two[...].astype(F32) + three[...].astype(F32)
    send[...] = total.astype(BF16)


def add_x(*parts):
    return pl.pallas_call(
        x_kernel,
        out_shape=jax.ShapeDtypeStruct((2, ROWS, OUT), BF16),
        in_specs=full(4),
        out_specs=full(1)[0],
        compiler_params=params(),
        name="add_x",
    )(*parts)


def sum_kernel(stay, two, three, one, got, plain, mirror, stays, stays_other):
    lane = lax.broadcasted_iota(jnp.int32, (ROWS, LANE), 1)
    pad = jnp.zeros((LANE - 2 * ROWS, LANE), F32)
    totals = []
    for pair in range(2):
        total = stay[pair]
        for part in (one, two, three, got):
            total = total + part[pair].astype(F32)
        totals.append(total)
    here = core_here() == 0
    ordered = (jnp.where(here, totals[0], totals[1]), jnp.where(here, totals[1], totals[0]))
    for at, total in enumerate(ordered):
        plain[at] = total[:, :WIDE]
        last = total[:, WIDE:]
        second = jnp.where(lane < 32, pltpu.roll(last, 32, 1), pltpu.roll(total[:, LANE:WIDE], 48, 1))
        turned = jnp.concatenate([last, second, pad], axis=0).T
        mirror[at] = turned[0:ROWS]
        (stays, stays_other)[at][...] = turned[ROWS:2 * ROWS]


def sum_parts(*parts):
    slim = jax.ShapeDtypeStruct((ROWS, LANE), F32)
    return pl.pallas_call(
        sum_kernel,
        out_shape=(jax.ShapeDtypeStruct((2, ROWS, WIDE), F32), jax.ShapeDtypeStruct((2, ROWS, LANE), F32), slim, slim),
        in_specs=full(5),
        out_specs=tuple(full(4)),
        compiler_params=params(),
        name="sum_parts",
    )(*parts)


def place_kernel(mirror, mirror_other, plain, plain_other, stays, stays_other, divisor, residual, update):
    row = lax.axis_index("row")
    z, y_lo = lax.div(row, 2), lax.rem(row, 2)
    here = core_here() == 0

    def both(near, far):
        return jnp.where(here, near, far), jnp.where(here, far, near)

    plain_0, plain_1 = both(plain[0], plain_other[...])
    mirror_0, mirror_1 = both(mirror[0], mirror_other[...])
    stays_0, stays_1 = stays[...], stays_other[...]

    def piece(array, at):
        return array[:, at * ROWS:(at + 1) * ROWS]

    wide = jnp.concatenate([
        piece(plain_0, 3), piece(plain_1, 4),
        piece(plain_0, 0), piece(mirror_1, 0),
        piece(plain_0, 1), piece(stays_1, 0),
        piece(plain_0, 2), piece(mirror_0, 1),
        piece(plain_0, 4), piece(plain_1, 3),
        piece(mirror_1, 1), piece(plain_1, 2),
        piece(stays_0, 0), piece(plain_1, 1),
        piece(mirror_0, 0), piece(plain_1, 0)], axis=1)
    count = wide.shape[1]
    even = lax.rem(lax.broadcasted_iota(jnp.int32, (1, count), 1), 2 * ROWS) < ROWS
    swapped = jnp.where(even, pltpu.roll(wide, count - ROWS, 1), pltpu.roll(wide, ROWS, 1))
    value = pltpu.roll(jnp.where(y_lo == 0, wide, swapped), z * (2 * ROWS), 1)
    residual[0] = value
    update[0] = value / divisor[...]


def place(*parts):
    out = jax.ShapeDtypeStruct((1, ROWS, 16 * ROWS), F32)
    return pl.pallas_call(
        place_kernel,
        out_shape=(out, out),
        in_specs=full(7),
        out_specs=tuple(full(2)),
        compiler_params=params(),
        name="place",
    )(*parts)


def weights_kernel(amplitudes, weights, held, arrived):
    copy = pltpu.make_async_copy(amplitudes, held, arrived)
    copy.start()
    column = lax.broadcasted_iota(jnp.int32, (1, DEPTH), 1)
    slab = lax.broadcasted_iota(jnp.int32, (SLAB, DEPTH), 0)
    within = lax.broadcasted_iota(jnp.int32, (PAIRS * GROUP, DEPTH), 0)
    same = lax.rem(within, GROUP) == lax.rem(column, GROUP)
    d, c = lax.div(column, SLAB * GROUP), lax.rem(lax.div(column, GROUP), SLAB)
    copy.wait()
    flat = held[...].reshape(SLAB * PAIRS, SLAB)
    for order, (outer, inner) in enumerate(((c, d), (d, c))):
        spread = jnp.where(slab == inner, 1.0, 0.0).astype(BF16)
        wide = jnp.dot(flat, spread, preferred_element_type=F32).reshape(SLAB, PAIRS, DEPTH)
        total = jnp.where(outer == 0, wide[0], 0.0)
        for at in range(1, SLAB):
            total = jnp.where(outer == at, wide[at], total)
        total = jnp.broadcast_to(total[:, None, :], (PAIRS, GROUP, DEPTH)).reshape(PAIRS * GROUP, DEPTH)
        weights[order * PAIRS * GROUP:(order + 1) * PAIRS * GROUP, :] = jnp.where(same, total, 0.0).astype(BF16)


def contraction_weights(amplitudes):
    return pl.pallas_call(
        weights_kernel,
        out_shape=jax.ShapeDtypeStruct((2 * PAIRS * GROUP, DEPTH), BF16),
        in_specs=[pl.BlockSpec(memory_space=pl.ANY)],
        out_specs=full(1)[0],
        scratch_shapes=[pltpu.VMEM((SLAB, PAIRS, SLAB), BF16), pltpu.SemaphoreType.DMA],
        compiler_params=params(),
        name="weights",
    )(jnp.transpose(amplitudes, (1, 0, 2)))


def per_device(factors, amplitudes, vir_energy, pair_energy):
    def moved(block, **by):
        return [shift(part, **by) for part in block]

    own = pack_block(factors)
    p1 = moved(own, dz=-1)
    m1 = moved(own, dz=1)
    weights = contraction_weights(amplitudes)
    p2 = moved(p1, dz=-1)
    m2 = moved(m1, dz=1)
    cross = moved(p2, dy=1)
    others = (*m1, *own, *p1, *m2, *p2)
    raw = first_star(others, weights)
    keep, send, products = second_star(cross, others, weights, raw)
    far = add_cores(keep, shift(send, dc=1))
    keep, send, divisor = last_star(products, weights, raw, vir_energy, pair_energy)
    near = add_cores(keep, shift(send, dc=1))

    def along_x(stay, one, two, three):
        return stay, shift(two, dx=2), shift(three, dx=-1), shift(one, dx=1)

    got = shift(add_x(*along_x(*far)), dh=1)
    plain, mirror, stays, stays_other = sum_parts(*along_x(*near), got)
    plain = to_rows(plain, ((-2, 0), (2, 1)))
    mirror = to_rows(mirror, ((-1, 0), (1, 0)))
    plain_other = shift(plain[1], dc=1)
    mirror_other = shift(mirror[1], dc=1)
    return place(mirror, mirror_other, plain, plain_other, stays, stays_other, divisor)


def solution(mesh):
    return jax.shard_map(
        per_device,
        mesh=mesh,
        in_specs=(P("row", None, "col"), P(), P(), P()),
        out_specs=(P("col", "row", None), P("col", "row", None)),
        check_vma=False,
    )
```
